128 devices in a mesh: section: 2 (over x_hi), dp: 4 (over y), expert: 16 (over x_lo, z, core).
Axes of the slice: x: 4 (x_hi: 2, x_lo: 2; x = x_hi * 2 + x_lo), y: 4, z: 4, core: 2. Of those that a mesh axis runs over, the one named last changes fastest.
Arguments:
- inputs: bfloat16 [2, 12608, 768], P(None, ('dp', 'expert')), may hold values from -6 to 6
- cotangent: bfloat16 [2, 12608, 768], P(None, ('dp', 'expert')), may hold values from -6 to 6
- qkv_weight: bfloat16 [2, 768, 2304], P('section', 'dp'), may hold values from -0.21875 to 0.21875
- attn_out_weight: bfloat16 [2, 768, 768], P('section', 'dp'), may hold values from -0.4375 to 0.4375
- router_weight: bfloat16 [2, 768, 16], P('section', 'dp'), may hold values from -0.109375 to 0.109375
- norm_params: bfloat16 [2, 4, 768], P('section', None, 'dp'), may hold values from -1 to 1.4, as said below
- expert_in: bfloat16 [2, 16, 768, 3072], P('section', 'expert', 'dp'), may hold values from -0.21875 to 0.21875
- expert_out: bfloat16 [2, 16, 3072, 768], P('section', 'expert', None, 'dp'), may hold values from -1.75 to 1.75
- routes: int32 [2, 2, 12608, 2], P('section', None, ('dp', 'expert')), may hold values from 0 to 15, as said below
- slots: int32 [2, 2, 12608, 2], P('section', None, ('dp', 'expert')), may hold values from 0 to 7, as said below
- kept: int32 [2, 2, 12608, 2], P('section', None, ('dp', 'expert')), may hold values from 0 to 1, as said below
Outputs:
- section_outputs: bfloat16 [2, 2, 12608, 768], P('section', None, ('dp', 'expert'))
- grad_inputs: float32 [2, 2, 12608, 768], P('section', None, ('dp', 'expert'))
- grad_qkv: float32 [2, 768, 2304], P('section', 'dp')
- grad_attn_out: float32 [2, 768, 768], P('section', 'dp')
- grad_router: float32 [2, 768, 16], P('section', 'dp')
- grad_norms: float32 [2, 4, 768], P('section', None, 'dp')
- grad_expert_in: float32 [2, 16, 768, 3072], P('section', 'expert', 'dp')
- grad_expert_out: float32 [2, 16, 3072, 768], P('section', 'expert', None, 'dp')
The draws below stay inside these ranges and needn't reach their ends.
Inputs may be any that keep to these rules, and one draw needn't show every extreme that they name: `routes`: the two experts of a token differ. For each section, micro-batch and index of dp, one expert is named by 8 + 1 or more first choices among the 197 tokens of every device with that index of dp. `slots`: within the 197 tokens of one device in one micro-batch of a section, an assignment's slot is the number of earlier assignments to the same expert, all first choices in token order coming before all second choices, capped at 7. `kept`: 1 exactly where the uncapped count of earlier assignments to the same expert (as for slots) is below 8, so that kept assignments of one device's tokens have distinct expert and slot. `norm_params`: rows 0 and 2 are gains, rows 1 and 3 shifts.
All inputs are finite; a program needn't handle non-finite values.
Results may differ from the reference program's by a relative error of at most 0.024.
Values may be sent and summed in bfloat16 or wider, within the bound.
No kernel may reach another device: no remote copies, remote signals or barrier semaphores. Data moves between devices by JAX's collectives and lax.ppermute only.
A program may use at most 192 MiB of HBM per device.

```python
import jax
import jax.numpy as jnp
from jax import lax

D = 768
HEADS = 12
HDIM = 64
FF = 3072
SEQ = 197
MICRO = 2
TOP = 2
SECTIONS = 2
EXPERTS = 16
TOK_MB = 197
CAP = 8
TOKENS = 12608
N_DP = 4
N_EXPERT = 16


def routing_tables(key):
    hot_key, coin_key, first_key, second_key, order_key = jax.random.split(key, 5)
    shape = (SECTIONS, MICRO, N_DP, N_EXPERT, TOK_MB)
    hot = jax.random.randint(hot_key, (SECTIONS, MICRO, N_DP, 1, 1), 0, EXPERTS)
    coin = jax.random.randint(coin_key, shape, 0, 4)
    first = jax.random.randint(first_key, shape, 0, EXPERTS)
    order_keys = jax.random.split(order_key, SECTIONS * MICRO * N_DP * N_EXPERT)
    order = jax.vmap(lambda single: jax.random.permutation(single, TOK_MB))(order_keys).reshape(shape)
    first = jnp.where((order < CAP + 1) | (coin == 0), hot, first)
    second = (first + jax.random.randint(second_key, shape, 1, EXPERTS)) % EXPERTS
    sequence = jnp.concatenate([first, second], axis=-1)
    onehot = (sequence[..., None] == jnp.arange(EXPERTS)).astype(jnp.int32)
    rank = jnp.sum((jnp.cumsum(onehot, axis=-2) - onehot) * onehot, axis=-1)
    both = jnp.stack([sequence[..., :TOK_MB], sequence[..., TOK_MB:]], axis=-1)
    ranks = jnp.stack([rank[..., :TOK_MB], rank[..., TOK_MB:]], axis=-1)
    flat = (SECTIONS, MICRO, N_DP * N_EXPERT * TOK_MB, TOP)
    places = jnp.minimum(ranks, CAP - 1)
    keeps = (ranks < CAP).astype(jnp.int32)
    return (both.reshape(flat).astype(jnp.int32), places.reshape(flat).astype(jnp.int32), keeps.reshape(flat))


def draw_routes(key, part):
    tables = routing_tables(key)
    return tables[0]


def draw_slots(key, part):
    tables = routing_tables(key)
    return tables[1]


def draw_kept(key, part):
    tables = routing_tables(key)
    return tables[2]


def draw_norm_params(key, part):
    key = jax.random.fold_in(key, 7)
    gain_key, shift_key = jax.random.split(key)
    gains = jax.random.uniform(gain_key, (SECTIONS, 2, 1, D), minval=0.6, maxval=1.4)
    shifts = jnp.clip(0.3 * jax.random.normal(shift_key, (SECTIONS, 2, 1, D)), -1.0, 1.0)
    return jnp.concatenate([gains, shifts], axis=2).reshape(SECTIONS, 4, D).astype(jnp.bfloat16)


def steps_of(stream_key, extent, shards, smallest, largest):
    factor_of = 1.0
    for axis_at, shards_of in shards:
        draws = jax.random.uniform(jax.random.fold_in(jax.random.fold_in(stream_key, 6), axis_at), (shards_of,), jnp.float32, smallest / len(shards), largest / len(shards))
        factor_of = factor_of * jnp.repeat(jnp.exp(draws), extent[axis_at] // shards_of).reshape((-1,) + (1,) * (len(extent) - 1 - axis_at))
    return factor_of


def normal_values(rng, extent, deviation, limit, shards=(), kind=jnp.bfloat16):
    factor_of = steps_of(rng, extent, shards, -0.22, 0.18) if shards else 1.0
    array = jax.random.normal(rng, extent, jnp.float32) * deviation * factor_of
    return jnp.minimum(jnp.maximum(array, -limit), limit).astype(kind)


def setup_inputs(seed: int = 0) -> dict:
    splits = jax.random.split(jax.random.key(seed), 12)
    inputs = normal_values(splits[0], (MICRO, TOKENS, D), 1.0, 6.0, ((1, 64),))
    cotangent = normal_values(splits[1], (MICRO, TOKENS, D), 1.0, 6.0, ((1, 64),))
    qkv_weight = normal_values(splits[2], (SECTIONS, D, 3 * D), D ** -0.5, 0.21875, ((0, 2), (1, 4)))
    attn_out_weight = normal_values(splits[3], (SECTIONS, D, D), (D // 4) ** -0.5, 0.4375, ((0, 2), (1, 4)))
    router_weight = normal_values(splits[4], (SECTIONS, D, EXPERTS), (4 * D) ** -0.5, 0.109375, ((0, 2), (1, 4)))
    norm_params = draw_norm_params(jax.random.fold_in(splits[11], 71), 0)
    expert_in = normal_values(splits[6], (SECTIONS, EXPERTS, D, FF), D ** -0.5, 0.21875, ((0, 2), (1, 16), (2, 4)))
    expert_out = normal_values(splits[7], (SECTIONS, EXPERTS, FF, D), (max(1, FF // (EXPERTS * EXPERTS))) ** -0.5, 1.75, ((0, 2), (1, 16), (3, 4)))
    routes = draw_routes(jax.random.fold_in(splits[11], 71), 0)
    slots = draw_slots(jax.random.fold_in(splits[11], 71), 0)
    kept = draw_kept(jax.random.fold_in(splits[11], 71), 0)
    return dict(inputs=inputs, cotangent=cotangent, qkv_weight=qkv_weight, attn_out_weight=attn_out_weight, router_weight=router_weight, norm_params=norm_params, expert_in=expert_in, expert_out=expert_out, routes=routes, slots=slots, kept=kept)


@jax.custom_vjp
def low(v):
    return lax.optimization_barrier(v.astype(jnp.bfloat16)).astype(jnp.float32)

@jax.custom_vjp
def low_back(v):
    return v

def low_keep(v):
    return (low(v), None)

def low_pass(kept, grad):
    return (grad,)

def back_keep(v):
    return (v, None)

def back_low(kept, grad):
    return (low(grad),)
low.defvjp(low_keep, low_pass)
low_back.defvjp(back_keep, back_low)
EPSILON = 1e-06
HIGH = lax.Precision.HIGHEST

def norm_rows(rows, gain, shift):
    centred = rows - lax.optimization_barrier(jnp.mean(rows, axis=-1, keepdims=True))
    spread = lax.optimization_barrier(jnp.mean(centred * centred, axis=-1, keepdims=True))
    return centred * lax.rsqrt(spread + EPSILON) * gain + shift

def layer(rows_in, wqkv, wout, wroute, norms, w_in, w_back, route, place, keep):
    count = rows_in.shape[0]
    blocks = count // TOK_MB
    normed = low(norm_rows(rows_in, norms[0], norms[1]))
    packed = low_back(low(jnp.dot(normed, wqkv, precision=HIGH)))
    split = packed.reshape(count // SEQ, SEQ, 3, HEADS, HDIM)
    scores = low_back(jnp.einsum('iqhd,ikhd->ihqk', split[:, :, 0], split[:, :, 1], precision=HIGH) * HDIM ** (-0.5))
    expo = jnp.exp(scores - lax.optimization_barrier(jnp.max(scores, axis=-1, keepdims=True)))
    attend = low(expo / lax.optimization_barrier(jnp.sum(expo, axis=-1, keepdims=True)))
    mixed = jnp.einsum('ihqk,ikhd->iqhd', attend, split[:, :, 2], precision=HIGH).reshape(count, D)
    mixed = low_back(low(mixed))
    middle = rows_in + low_back(jnp.dot(mixed, wout, precision=HIGH))
    second = low(norm_rows(middle, norms[2], norms[3]))
    logits = low_back(jnp.dot(second, wroute, precision=HIGH))
    gate_all = jax.nn.softmax(logits, axis=-1)
    chosen = route.reshape(blocks, TOK_MB, TOP).astype(jnp.int32)
    slot = place.reshape(blocks, TOK_MB, TOP).astype(jnp.int32)
    live = keep.reshape(blocks, TOK_MB, TOP).astype(jnp.float32)
    owner = jnp.arange(blocks).astype(jnp.int32)[:, None, None]
    buffer = jnp.zeros((blocks, EXPERTS, CAP, D), jnp.float32)
    buffer = buffer.at[owner, chosen, slot].add(live[..., None] * second.reshape(blocks, TOK_MB, 1, D))
    buffer = low_back(buffer)
    pre = low_back(jnp.einsum('becd,edf->becf', buffer, w_in, precision=HIGH))
    hidden = low(jax.nn.gelu(pre, approximate=False))
    answers = low_back(low(jnp.einsum('becf,efd->becd', hidden, w_back, precision=HIGH)))
    picked = answers[owner, chosen, slot]
    gates = jnp.take_along_axis(gate_all.reshape(blocks, TOK_MB, EXPERTS), chosen, axis=-1) * live
    return middle + lax.optimization_barrier(jnp.sum(gates[..., None] * picked, axis=2)).reshape(count, D)

def section(rows_all, wqkv, wout, wroute, norms, w_in, w_back, route, place, keep):
    results = [layer(rows_all[index], wqkv, wout, wroute, norms, w_in, w_back, route[index], place[index], keep[index]) for index in range(MICRO)]
    return jnp.stack(results)

def reference(inputs, cotangent, qkv_weight, attn_out_weight, router_weight, norm_params, expert_in, expert_out, routes, slots, kept):
    weights = (qkv_weight, attn_out_weight, router_weight, norm_params, expert_in, expert_out)

    def runner(level):

        def apply(rows_all, wqkv, wout, wroute, norms, w_in, w_back):
            return section(rows_all, wqkv, wout, wroute, norms, w_in, w_back, routes[level], slots[level], kept[level])
        return apply
    params_zero = [weight[0].astype(jnp.float32) for weight in weights]
    params_one = [weight[1].astype(jnp.float32) for weight in weights]
    first, pull_first = jax.vjp(runner(0), inputs.astype(jnp.float32), *params_zero)
    passed = low(first)
    second, pull_second = jax.vjp(runner(1), passed, *params_one)
    back_second = pull_second(cotangent.astype(jnp.float32))
    back_first = pull_first(low(back_second[0]))
    outputs = jnp.stack([first, second]).astype(jnp.bfloat16)
    grad_in = jnp.stack([back_first[0], back_second[0]])
    grads = [jnp.stack([back_first[number], back_second[number]]) for number in range(1, 7)]
    return (outputs, grad_in, grads[0], grads[1], grads[2], grads[3], grads[4], grads[5])
```

```python
import functools

import jax
import jax.numpy as jnp
from jax import lax
from jax.experimental import pallas as pl
from jax.experimental.pallas import tpu as pltpu
from jax.sharding import PartitionSpec as P

WIDTH = 768
HDIM = 64
SEQ = 197
ROWS = 208
EXPERTS = 16
SLOTS = 8
PLACES = EXPERTS * SLOTS
HIDDEN = 3072
EPSILON = 1e-06
SCALE = HDIM ** (-0.5)
PAIRS = WIDTH // (2 * HDIM)
HALF = 1536
EXTRA = 128
WIDE = HALF + EXTRA
BLOCK = 512
STEPS = HIDDEN // BLOCK
VMEM = 50 * 1024 * 1024
SECTION_EXPERT = ("section", "expert")

bf16 = jnp.bfloat16
f32 = jnp.float32


def mm(a, b, contract=(1, 0)):
    return lax.dot_general(
        a, b, (((contract[0],), (contract[1],)), ((), ())), preferred_element_type=f32
    )


def normalize(rows):
    centred = rows - jnp.mean(rows, axis=-1, keepdims=True)
    factor = lax.rsqrt(jnp.mean(centred * centred, axis=-1, keepdims=True) + EPSILON)
    return centred * factor, factor


def norm_backward(grad, normal, factor, gain):
    scaled = grad * gain
    inner = (
        scaled
        - jnp.mean(scaled, axis=-1, keepdims=True)
        - normal * jnp.mean(scaled * normal, axis=-1, keepdims=True)
    )
    return factor * inner


def gelu_parts(pre):
    cdf = 0.5 * (1.0 + lax.erf(pre * 0.7071067811865476))
    return cdf


def gelu_slope(pre, cdf):
    return cdf + pre * (0.3989422804014327 * jnp.exp(-0.5 * pre * pre))


def extras_of(wa_ref):
    turned = wa_ref[:, HALF:WIDE].astype(f32).T
    return turned


def selection(target_ref):
    places = lax.broadcasted_iota(jnp.int32, (PLACES, ROWS), 0)
    return (places == target_ref[0:1, :]) | (places == target_ref[1:2, :])


def slot_gates(chosen, gate_t):
    spread = jnp.broadcast_to(gate_t[:, None, :], (EXPERTS, SLOTS, ROWS)).reshape(PLACES, ROWS)
    return jnp.sum(jnp.where(chosen, spread, 0.0), axis=1, keepdims=True)


def low_lanes():
    return lax.broadcasted_iota(jnp.int32, (ROWS, 2 * HDIM), 1) < HDIM


def combine(middle, chosen, gate_t, answers):
    weighted = slot_gates(chosen, gate_t) * answers
    high = weighted.astype(bf16)
    low = (weighted - high.astype(f32)).astype(bf16)
    pick = chosen.astype(f32).astype(bf16)
    return middle + mm(pick, high, (0, 0)) + mm(pick, low, (0, 0))


def attention_forward(
    rows, wa_ref, wb_ref, target_ref, packed_ref, mixed_ref, middle_ref, logsum_ref, gate_ref
):
    extras = extras_of(wa_ref)
    normal, _ = normalize(rows)
    normed = (normal * extras[16:17] + extras[17:18]).astype(bf16)
    for start in range(0, HALF, WIDTH):
        packed_ref[:, start : start + WIDTH] = mm(normed, wa_ref[:, start : start + WIDTH]).astype(
            bf16
        )
    packed_ref[:, HALF:] = mm(normed, wb_ref[:, :WIDTH]).astype(bf16)
    lower = low_lanes()
    inside = lax.broadcasted_iota(jnp.int32, (ROWS, ROWS), 1) < SEQ
    lanes = lax.broadcasted_iota(jnp.int32, (ROWS, 128), 1)
    logsums = jnp.zeros((ROWS, 128), f32)
    for pair in range(PAIRS):
        at = pair * 128
        queries = packed_ref[:, at : at + 128]
        keys = packed_ref[:, WIDTH + at : WIDTH + at + 128]
        values = packed_ref[:, 2 * WIDTH + at : 2 * WIDTH + at + 128]
        outs = []
        for side in range(2):
            mine = lower if side == 0 else jnp.logical_not(lower)
            scores = mm(jnp.where(mine, queries, jnp.zeros_like(queries)), keys, (1, 1)) * SCALE
            scores = jnp.where(inside, scores, -1e30)
            highest = jnp.max(scores, axis=-1, keepdims=True)
            expo = jnp.exp(scores - highest)
            total = jnp.sum(expo, axis=-1, keepdims=True)
            logsums = jnp.where(lanes == 2 * pair + side, highest + jnp.log(total), logsums)
            attend = (expo * (1.0 / total)).astype(bf16)
            outs.append(mm(attend, values))
        mixed_ref[:, at : at + 128] = jnp.where(lower, outs[0], outs[1]).astype(bf16)
    logsum_ref[...] = logsums
    middle = rows + mm(mixed_ref[...], wb_ref[:, WIDTH:HALF])
    middle_ref[...] = middle
    normal, _ = normalize(middle)
    second = (normal * extras[18:19] + extras[19:20]).astype(bf16)
    logits = mm(extras[0:EXPERTS].astype(bf16), second, (1, 1))
    expo = jnp.exp(logits - jnp.max(logits, axis=0, keepdims=True))
    gate_t = expo / jnp.sum(expo, axis=0, keepdims=True)
    gate_ref[...] = gate_t
    chosen = selection(target_ref)
    buffer = mm(chosen.astype(f32).astype(bf16), second)
    return chosen, gate_t, buffer


def attention_backward(
    which, grad_out, rows, answers, grad_buffer, target_ref, gate_ref, middle_ref, mixed_ref,
    packed_ref, logsum_ref, wa_ref, wb_ref, mine_ref, send_ref, mixed_grad_ref, packed_grad_ref,
):
    def put(half, start, value):
        value = value.astype(bf16)
        columns = slice(start, start + value.shape[1])

        @pl.when(which == half)
        def _():
            mine_ref[:, columns] = value

        @pl.when(which != half)
        def _():
            send_ref[:, columns] = value

    extras = extras_of(wa_ref)
    gate_t = gate_ref[...]
    chosen = selection(target_ref)
    pick_wide = chosen.astype(f32)
    pick = pick_wide.astype(bf16)
    arrived = mm(pick, grad_out.astype(bf16))
    grad_gates = jnp.sum(arrived * answers, axis=1, keepdims=True)
    grad_probs = jnp.sum((pick_wide * grad_gates).reshape(EXPERTS, SLOTS, ROWS), axis=1)
    grad_logits = gate_t * (grad_probs - jnp.sum(grad_probs * gate_t, axis=0, keepdims=True))
    grad_logits = grad_logits.astype(bf16)
    normal, factor = normalize(middle_ref[...])
    second = (normal * extras[18:19] + extras[19:20]).astype(bf16)
    grad_router = mm(grad_logits, second)
    grad_second = mm(grad_logits, extras[0:EXPERTS].astype(bf16), (0, 0)) + mm(
        pick, grad_buffer, (0, 0)
    )
    gain_two = jnp.sum(grad_second * normal, axis=0, keepdims=True)
    shift_two = jnp.sum(grad_second, axis=0, keepdims=True)
    grad_middle = grad_out + norm_backward(grad_second, normal, factor, extras[18:19])
    branch = grad_middle.astype(bf16)
    put(1, WIDTH, mm(mixed_ref[...], branch, (0, 0)))
    mixed_grad_ref[...] = mm(branch, wb_ref[:, WIDTH:HALF], (1, 1)).astype(bf16)
    lower = low_lanes()
    inside = lax.broadcasted_iota(jnp.int32, (ROWS, ROWS), 1) < SEQ
    for pair in range(PAIRS):
        at = pair * 128
        queries = packed_ref[:, at : at + 128]
        keys = packed_ref[:, WIDTH + at : WIDTH + at + 128]
        values = packed_ref[:, 2 * WIDTH + at : 2 * WIDTH + at + 128]
        upstream = mixed_grad_ref[:, at : at + 128]
        sums = [0.0, 0.0, 0.0]
        for side in range(2):
            mine = lower if side == 0 else jnp.logical_not(lower)
            zero = jnp.zeros_like(queries)
            queries_one = jnp.where(mine, queries, zero)
            upstream_one = jnp.where(mine, upstream, zero)
            scores = mm(queries_one, keys, (1, 1)) * SCALE
            head = 2 * pair + side
            attend = jnp.exp(scores - logsum_ref[:, head : head + 1])
            attend = jnp.where(inside, attend, 0.0)
            grad_attend = mm(upstream_one, values, (1, 1))
            inner = jnp.sum(grad_attend * attend, axis=-1, keepdims=True)
            grad_scores = (attend * (grad_attend - inner)).astype(bf16)
            sums[0] += mm(grad_scores, jnp.where(mine, keys, zero))
            sums[1] += mm(grad_scores, queries_one, (0, 0))
            sums[2] += mm(attend.astype(bf16), upstream_one, (0, 0))
        packed_grad_ref[:, at : at + 128] = (sums[0] * SCALE).astype(bf16)
        packed_grad_ref[:, WIDTH + at : WIDTH + at + 128] = (sums[1] * SCALE).astype(bf16)
        packed_grad_ref[:, 2 * WIDTH + at : 2 * WIDTH + at + 128] = sums[2].astype(bf16)
    normal, factor = normalize(rows)
    normed = (normal * extras[16:17] + extras[17:18]).astype(bf16)
    put(0, 0, mm(normed, packed_grad_ref[:, 0:WIDTH], (0, 0)))
    put(0, WIDTH, mm(normed, packed_grad_ref[:, WIDTH:HALF], (0, 0)))
    put(1, 0, mm(normed, packed_grad_ref[:, HALF:], (0, 0)))
    grad_normed = mm(packed_grad_ref[:, :HALF], wa_ref[:, :HALF], (1, 1)) + mm(
        packed_grad_ref[:, HALF:], wb_ref[:, :WIDTH], (1, 1)
    )
    gain_one = jnp.sum(grad_normed * normal, axis=0, keepdims=True)
    shift_one = jnp.sum(grad_normed, axis=0, keepdims=True)
    small = jnp.concatenate(
        [
            grad_router,
            gain_one,
            shift_one,
            gain_two,
            shift_two,
            jnp.zeros((EXTRA - EXPERTS - 4, WIDTH), f32),
        ],
        axis=0,
    )
    put(0, HALF, small.T)
    put(1, HALF, jnp.zeros((WIDTH, EXTRA), f32))
    return grad_middle + norm_backward(grad_normed, normal, factor, extras[16:17])


def fetch(which, own_ref, other_ref, wa_ref, wb_ref, sems):
    @pl.when(which == 0)
    def _():
        pltpu.make_async_copy(own_ref, wa_ref, sems.at[0]).start()
        pltpu.make_async_copy(other_ref, wb_ref, sems.at[1]).start()

    @pl.when(which != 0)
    def _():
        pltpu.make_async_copy(other_ref, wa_ref, sems.at[0]).start()
        pltpu.make_async_copy(own_ref, wb_ref, sems.at[1]).start()

    pltpu.make_async_copy(own_ref, wa_ref, sems.at[0]).wait()
    pltpu.make_async_copy(other_ref, wb_ref, sems.at[1]).wait()


def first_kernel(
    which_ref, own_ref, other_ref, rows_ref, target_ref,
    packed_ref, mixed_ref, middle_ref, logsum_ref, gate_ref, send_ref, wa_ref, wb_ref, sems,
):
    fetch(which_ref[0], own_ref, other_ref, wa_ref, wb_ref, sems)
    _, _, buffer = attention_forward(
        rows_ref[...].astype(f32), wa_ref, wb_ref, target_ref,
        packed_ref, mixed_ref, middle_ref, logsum_ref, gate_ref,
    )
    send_ref[0:PLACES] = buffer.astype(bf16)
    send_ref[PLACES:] = jnp.zeros((PLACES, WIDTH), bf16)


def second_kernel(
    which_ref, own_ref, other_ref, middle_in_ref, gate_in_ref, target_in_ref, answers_ref, grad_ref,
    target_ref,
    out_ref, packed_ref, mixed_ref, middle_ref, logsum_ref, gate_ref, send_ref, wa_ref, wb_ref, sems,
):
    fetch(which_ref[0], own_ref, other_ref, wa_ref, wb_ref, sems)
    out = combine(
        middle_in_ref[...],
        selection(target_in_ref),
        gate_in_ref[...],
        answers_ref[...].astype(f32),
    )
    out_ref[...] = out.astype(bf16)
    chosen, gate_t, buffer = attention_forward(
        out.astype(bf16).astype(f32), wa_ref, wb_ref, target_ref,
        packed_ref, mixed_ref, middle_ref, logsum_ref, gate_ref,
    )
    arrived = mm(chosen.astype(f32).astype(bf16), grad_ref[...])
    grad_answers = slot_gates(chosen, gate_t) * arrived
    both = jnp.concatenate(
        [
            buffer.reshape(EXPERTS, SLOTS, WIDTH),
            grad_answers.reshape(EXPERTS, SLOTS, WIDTH),
        ],
        axis=1,
    ).reshape(2 * PLACES, WIDTH)
    send_ref[0 : 2 * PLACES] = jnp.zeros((2 * PLACES, WIDTH), bf16)
    send_ref[2 * PLACES :] = both.astype(bf16)


def third_kernel(
    which_ref, own_ref, other_ref, back_ref, grad_ref, rows_ref, target_ref, gate_ref, middle_ref,
    mixed_ref, packed_ref, logsum_ref, target_next_ref, gate_next_ref,
    out_ref, grad_in_ref, grad_low_ref, send_ref, mine_ref, other_grad_ref,
    wa_ref, wb_ref, sems, mixed_grad_ref, packed_grad_ref,
):
    fetch(which_ref[0], own_ref, other_ref, wa_ref, wb_ref, sems)
    back = back_ref[...].astype(f32).reshape(EXPERTS, 2 * SLOTS, WIDTH)
    answers = back[:, :SLOTS].reshape(PLACES, WIDTH)
    grad_buffer = back[:, SLOTS:].reshape(PLACES, WIDTH).astype(bf16)
    out = combine(middle_ref[...], selection(target_ref), gate_ref[...], answers)
    out_ref[...] = out.astype(bf16)
    grad_in = attention_backward(
        which_ref[0], grad_ref[...].astype(f32), rows_ref[...].astype(f32), answers, grad_buffer,
        target_ref, gate_ref, middle_ref, mixed_ref, packed_ref, logsum_ref, wa_ref, wb_ref,
        mine_ref, other_grad_ref, mixed_grad_ref, packed_grad_ref,
    )
    grad_in_ref[...] = grad_in
    grad_low = grad_in.astype(bf16)
    grad_low_ref[...] = grad_low
    chosen = selection(target_next_ref)
    arrived = mm(chosen.astype(f32).astype(bf16), grad_low)
    send_ref[0:PLACES] = (slot_gates(chosen, gate_next_ref[...]) * arrived).astype(bf16)
    send_ref[PLACES:] = jnp.zeros((PLACES, WIDTH), bf16)


def last_kernel(
    which_ref, own_ref, other_ref, answers_ref, grad_buffer_ref, grad_ref, rows_ref, target_ref,
    gate_ref, middle_ref, mixed_ref, packed_ref, logsum_ref,
    grad_in_ref, mine_ref, other_grad_ref, wa_ref, wb_ref, sems, mixed_grad_ref, packed_grad_ref,
):
    fetch(which_ref[0], own_ref, other_ref, wa_ref, wb_ref, sems)
    grad_in_ref[...] = attention_backward(
        which_ref[0], grad_ref[...].astype(f32), rows_ref[...].astype(f32),
        answers_ref[...].astype(f32), grad_buffer_ref[...], target_ref, gate_ref, middle_ref,
        mixed_ref, packed_ref, logsum_ref, wa_ref, wb_ref,
        mine_ref, other_grad_ref, mixed_grad_ref, packed_grad_ref,
    )


def shape(*sizes, kind=bf16):
    return jax.ShapeDtypeStruct(sizes, kind)


SAVED = (
    shape(ROWS, 3 * WIDTH),
    shape(ROWS, WIDTH),
    shape(ROWS, WIDTH, kind=f32),
    shape(ROWS, 128, kind=f32),
    shape(EXPERTS, ROWS, kind=f32),
)
WEIGHT_SCRATCH = [
    pltpu.VMEM((WIDTH, WIDE), bf16),
    pltpu.VMEM((WIDTH, WIDE), bf16),
    pltpu.SemaphoreType.DMA((2,)),
]
GRAD_SCRATCH = [pltpu.VMEM((ROWS, WIDTH), bf16), pltpu.VMEM((ROWS, 3 * WIDTH), bf16)]


def whole(kernel, outs, scratch=(), flops=4e9):
    def call(*args):
        memories = [pltpu.SMEM, pl.ANY, pl.ANY] + [pltpu.VMEM] * (len(args) - 3)
        return pl.pallas_call(
            kernel,
            out_shape=outs,
            in_specs=[pl.BlockSpec(memory_space=space) for space in memories],
            out_specs=tuple(pl.BlockSpec(memory_space=pltpu.VMEM) for _ in outs),
            scratch_shapes=WEIGHT_SCRATCH + list(scratch),
            compiler_params=pltpu.CompilerParams(vmem_limit_bytes=VMEM),
            cost_estimate=pl.CostEstimate(
                flops=int(flops), bytes_accessed=12_000_000, transcendentals=600_000
            ),
        )(*args)

    return call


ITEMS = 2 * EXPERTS * SLOTS


def answer_kernel(items_ref, w_in_ref, w_back_ref, out_ref, total):
    step = pl.program_id(0)
    pre = mm(items_ref[...], w_in_ref[...])
    hidden = (pre * gelu_parts(pre)).astype(bf16)
    part = mm(hidden, w_back_ref[...], (1, 1))

    @pl.when(step == 0)
    def _():
        total[...] = part

    @pl.when(step > 0)
    def _():
        total[...] += part

    @pl.when(step == STEPS - 1)
    def _():
        out_ref[...] = total[...].astype(bf16)


def both_kernel(mixed_ref, w_in_ref, w_back_ref, out_ref, items, grads, total, total_grad):
    step = pl.program_id(0)

    @pl.when(step == 0)
    def _():
        rows = mixed_ref[...].astype(f32).reshape(ITEMS // SLOTS, 2 * SLOTS, WIDTH)
        items[...] = rows[:, :SLOTS].reshape(ITEMS, WIDTH).astype(bf16)
        grads[...] = rows[:, SLOTS:].reshape(ITEMS, WIDTH).astype(bf16)
        total[...] = jnp.zeros_like(total)
        total_grad[...] = jnp.zeros_like(total_grad)

    pre = mm(items[...], w_in_ref[...])
    cdf = gelu_parts(pre)
    total[...] += mm((pre * cdf).astype(bf16), w_back_ref[...], (1, 1))
    grad_hidden = mm(grads[...], w_back_ref[...])
    grad_pre = (grad_hidden * gelu_slope(pre, cdf)).astype(bf16)
    total_grad[...] += mm(grad_pre, w_in_ref[...], (1, 1))

    @pl.when(step == STEPS - 1)
    def _():
        both = jnp.concatenate(
            [
                total[...].reshape(ITEMS // SLOTS, SLOTS, WIDTH),
                total_grad[...].reshape(ITEMS // SLOTS, SLOTS, WIDTH),
            ],
            axis=1,
        )
        out_ref[...] = both.reshape(2 * ITEMS, WIDTH).astype(bf16)


def grads_kernel(items_ref, grads_ref, w_in_ref, w_back_ref, out_ref, weights_ref, total):
    step = pl.program_id(0)
    items, grads = items_ref[...], grads_ref[...]
    pre = mm(items, w_in_ref[...])
    cdf = gelu_parts(pre)
    hidden = (pre * cdf).astype(bf16)
    grad_hidden = mm(grads, w_back_ref[...])
    grad_pre = (grad_hidden * gelu_slope(pre, cdf)).astype(bf16)
    weights_ref[:, :BLOCK] = mm(items, grad_pre, (0, 0)).astype(bf16)
    weights_ref[:, BLOCK:] = mm(grads, hidden, (0, 0)).astype(bf16)
    part = mm(grad_pre, w_in_ref[...], (1, 1))

    @pl.when(step == 0)
    def _():
        total[...] = part

    @pl.when(step > 0)
    def _():
        total[...] += part

    @pl.when(step == STEPS - 1)
    def _():
        out_ref[...] = total[...].astype(bf16)


def spread_kernel(sum_ref, in_ref, out_ref):
    in_ref[...] = sum_ref[:, :BLOCK].astype(f32)
    out_ref[...] = sum_ref[:, BLOCK:].astype(f32).T


def expert_outputs(total):
    rows = total.shape[0]
    return pl.pallas_call(
        spread_kernel,
        grid=(STEPS,),
        out_shape=(shape(rows, HIDDEN, kind=f32), shape(HIDDEN, rows, kind=f32)),
        in_specs=[pl.BlockSpec((rows, 2 * BLOCK), lambda j: (0, j))],
        out_specs=(
            pl.BlockSpec((rows, BLOCK), lambda j: (0, j)),
            pl.BlockSpec((BLOCK, rows), lambda j: (j, 0)),
        ),
        cost_estimate=pl.CostEstimate(flops=0, bytes_accessed=7_000_000, transcendentals=0),
    )(total)


def expert_call(kernel, rows, weights, outs, out_specs, scratch, flops):
    return pl.pallas_call(
        kernel,
        grid=(STEPS,),
        out_shape=outs,
        in_specs=[pl.BlockSpec(each.shape, lambda j: (0, 0)) for each in rows]
        + [
            pl.BlockSpec((WIDTH, BLOCK), lambda j: (0, j)),
            pl.BlockSpec((WIDTH, BLOCK), lambda j: (0, j + STEPS)),
        ],
        out_specs=out_specs,
        scratch_shapes=scratch,
        compiler_params=pltpu.CompilerParams(vmem_limit_bytes=VMEM),
        cost_estimate=pl.CostEstimate(
            flops=int(flops), bytes_accessed=12_000_000, transcendentals=800_000
        ),
    )(*rows, weights, weights)


def resident(rows):
    return pl.BlockSpec((rows, WIDTH), lambda j: (0, 0))


def expert_answers(items, weights):
    return expert_call(
        answer_kernel, (items,), weights, shape(ITEMS, WIDTH), resident(ITEMS),
        [pltpu.VMEM((ITEMS, WIDTH), f32)], 2.4e9,
    )


def expert_both(mixed, weights):
    return expert_call(
        both_kernel, (mixed,), weights, shape(2 * ITEMS, WIDTH), resident(2 * ITEMS),
        [pltpu.VMEM((ITEMS, WIDTH), bf16)] * 2 + [pltpu.VMEM((ITEMS, WIDTH), f32)] * 2, 4.8e9,
    )


def expert_grads(items, grads, weights):
    return expert_call(
        grads_kernel, (items, grads), weights,
        (shape(ITEMS, WIDTH), shape(WIDTH, 2 * HIDDEN)),
        (resident(ITEMS), pl.BlockSpec((WIDTH, 2 * BLOCK), lambda j: (0, j))),
        [pltpu.VMEM((ITEMS, WIDTH), f32)], 6e9,
    )


def swap_sections(array):
    return lax.ppermute(array, "section", [(0, 1), (1, 0)])


def swap_cores(array):
    return lax.ppermute(array, "expert", [(i, i ^ 1) for i in range(EXPERTS)])


def shuffle(rows):
    return lax.all_to_all(rows, SECTION_EXPERT, split_axis=0, concat_axis=0, tiled=True)


def gather_rows(piece, me, axis, shifted):
    sizes = list(piece.shape)
    sizes.insert(axis, 4)
    out = jnp.zeros(sizes, piece.dtype)

    def place(out, got, at):
        start = [0] * len(sizes)
        start[axis] = at
        return lax.dynamic_update_slice(out, jnp.expand_dims(got, axis), start)

    out = place(out, piece, me)
    for by in (1, 3, 2):
        out = place(out, shifted(piece, by), (me - by) % 4)
    return out


def shift_dp(array, by):
    return lax.ppermute(array, "dp", [(i, (i + by) % 4) for i in range(4)])


def shift_z(array, by):
    pairs = [(i, i // 8 * 8 + (i % 8 + 2 * by) % 8) for i in range(EXPERTS)]
    return lax.ppermute(array, "expert", pairs)


SAME_CORE = [[core + 2 * i for i in range(8)] for core in (0, 1)]


def after(array, *earlier):
    return lax.optimization_barrier((array, *earlier))[0]


def add_cores(mine, send):
    half = mine.astype(f32) + swap_cores(send).astype(f32)
    return half.astype(bf16).reshape(4, 8, 24, WIDE).transpose(1, 0, 2, 3)


def add_group(parts):
    got = lax.all_to_all(
        parts, "expert", split_axis=0, concat_axis=0, tiled=True, axis_index_groups=SAME_CORE
    )
    return jnp.sum(got.astype(f32), axis=0).astype(bf16)


def shards(
    inputs, cotangent, qkv_weight, attn_out_weight, router_weight, norm_params, expert_in,
    expert_out, routes, slots, kept,
):
    first = lax.axis_index("section") == 0
    core = lax.rem(lax.axis_index("expert"), 2)
    even = core == 0
    which = core.reshape(1).astype(jnp.int32)

    def pick(zero, one):
        return jnp.where(first, zero, one)

    expert_shard = jnp.concatenate([expert_in[0, 0], expert_out[0, 0].T], axis=1)
    expert_weights = lax.all_gather(expert_shard, "dp", axis=0, tiled=True)

    extra = jnp.concatenate(
        [
            router_weight[0],
            norm_params[0].T,
            jnp.zeros((router_weight.shape[1], EXTRA - EXPERTS - 4), bf16),
        ],
        axis=1,
    )
    mine = jnp.concatenate(
        [
            jnp.where(
                even,
                qkv_weight[0][:, :HALF],
                jnp.concatenate([qkv_weight[0][:, HALF:], attn_out_weight[0]], axis=1),
            ),
            extra,
        ],
        axis=1,
    )
    dp = lax.axis_index("dp")
    z = lax.rem(lax.axis_index("expert"), 8) // 2
    mine = lax.dynamic_slice(mine, (z * 48, 0), (48, WIDE))
    theirs = swap_sections(mine)

    def halves(piece):
        over_dp = gather_rows(piece, dp, 0, shift_dp)
        own = gather_rows(over_dp, z, 1, shift_z).reshape(WIDTH, WIDE)
        return which, own, swap_cores(own)

    weights_one = halves(pick(mine, theirs))

    target = jnp.where(kept[0] > 0, routes[0] * SLOTS + slots[0], -1)
    target = jnp.pad(
        target.transpose(0, 2, 1), ((0, 0), (0, 0), (0, ROWS - SEQ)), constant_values=-1
    )
    received = swap_sections(pick(target[1], target[0]))
    own = pick(target[0], target[1])
    target_one, target_two = pick(own, received), pick(received, own)

    edge = ((0, ROWS - SEQ), (0, 0))
    rows_one = jnp.pad(pick(inputs[0], inputs[1]), edge)
    grad_two = jnp.pad(pick(cotangent[0], cotangent[1]), edge)

    packed_1, mixed_1, middle_1, logsum_1, gate_1, send = whole(
        first_kernel, SAVED + (shape(2 * PLACES, WIDTH),)
    )(*weights_one, rows_one, target_one)
    weights_two = halves(after(pick(theirs, mine), send))
    items_1 = shuffle(send.reshape(32, SLOTS, WIDTH)).reshape(ITEMS, WIDTH)
    answers = expert_answers(items_1, expert_weights)
    answers_1 = shuffle(answers.reshape(32, SLOTS, WIDTH))[:EXPERTS].reshape(PLACES, WIDTH)

    rows_two, packed_2, mixed_2, middle_2, logsum_2, gate_2, send = whole(
        second_kernel, (shape(ROWS, WIDTH),) + SAVED + (shape(4 * PLACES, WIDTH),)
    )(*weights_two, middle_1, gate_1, target_one, answers_1, grad_two, target_two)
    items_2 = shuffle(send.reshape(32, 2 * SLOTS, WIDTH))
    back = expert_both(items_2.reshape(2 * ITEMS, WIDTH), expert_weights)
    back = shuffle(back.reshape(32, 2 * SLOTS, WIDTH))[EXPERTS:].reshape(2 * PLACES, WIDTH)
    out_two, grad_in_two, grad_one, send, mine_2, other_2 = whole(
        third_kernel,
        (
            shape(ROWS, WIDTH),
            shape(ROWS, WIDTH, kind=f32),
            shape(ROWS, WIDTH),
            shape(2 * PLACES, WIDTH),
            shape(WIDTH, WIDE),
            shape(WIDTH, WIDE),
        ),
        scratch=GRAD_SCRATCH,
        flops=8e9,
    )(
        *weights_two, back, grad_two, rows_two, target_two, gate_2, middle_2, mixed_2, packed_2,
        logsum_2, target_one, gate_1,
    )

    grads_1 = shuffle(send.reshape(32, SLOTS, WIDTH))
    items = pick(items_1.reshape(32, SLOTS, WIDTH), items_2[:, :SLOTS]).reshape(ITEMS, WIDTH)
    grads = pick(grads_1, items_2[:, SLOTS:]).reshape(ITEMS, WIDTH)
    summed_2 = add_group(after(add_cores(mine_2, other_2), grads))
    back, expert_pair = expert_grads(items, grads, expert_weights)
    grad_buffer = shuffle(back.reshape(32, SLOTS, WIDTH))[:EXPERTS].reshape(PLACES, WIDTH)
    expert_sum = lax.psum_scatter(expert_pair, "dp", scatter_dimension=0, tiled=True)
    grad_in_one, mine_1, other_1 = whole(
        last_kernel,
        (shape(ROWS, WIDTH, kind=f32), shape(WIDTH, WIDE), shape(WIDTH, WIDE)),
        scratch=GRAD_SCRATCH,
        flops=8e9,
    )(
        *weights_one, answers_1, grad_buffer, grad_one, rows_one, target_one, gate_1, middle_1,
        mixed_1, packed_1, logsum_1,
    )

    def both_micros(zero, one, kind):
        zero, one = zero[:SEQ], one[:SEQ]
        got = swap_sections(pick(one, zero).astype(bf16)).astype(kind)
        local = pick(zero, one).astype(kind)
        return jnp.stack([pick(local, got), pick(got, local)])[None]

    section_outputs = both_micros(rows_two, out_two, bf16)
    grad_inputs = both_micros(grad_in_one, grad_in_two, f32)

    parts = jnp.stack([add_group(add_cores(mine_1, other_1)), summed_2])
    got = lax.all_to_all(
        parts.reshape(8, 24, WIDE), ("section", "dp"), split_axis=0, concat_axis=0, tiled=True
    )
    total = jnp.sum(got.astype(f32), axis=0).astype(bf16)
    own = lax.all_to_all(
        jnp.broadcast_to(total[None], (8, 24, WIDE)),
        "expert", split_axis=0, concat_axis=0, tiled=True, axis_index_groups=SAME_CORE,
    ).reshape(192, WIDE)
    other = swap_cores(own)
    half_a = jnp.where(even, own, other).astype(f32)
    half_b = jnp.where(even, other, own).astype(f32)
    grad_qkv = jnp.concatenate([half_a[:, :HALF], half_b[:, :WIDTH]], axis=1)
    grad_out = half_b[:, WIDTH:HALF]
    grad_router = half_a[:, HALF : HALF + EXPERTS]
    grad_norms = half_a[:, HALF + EXPERTS : HALF + EXPERTS + 4].T

    grad_expert_in, grad_expert_out = expert_outputs(expert_sum)
    return (
        section_outputs,
        grad_inputs,
        grad_qkv[None],
        grad_out[None],
        grad_router[None],
        grad_norms[None],
        grad_expert_in[None, None],
        grad_expert_out[None, None],
    )


def solution(mesh):
    tokens = P(None, ("dp", "expert"), None)
    tables = P("section", None, ("dp", "expert"), None)
    rows = P("section", "dp", None)
    norms = P("section", None, "dp")
    into = P("section", "expert", "dp", None)
    back = P("section", "expert", None, "dp")
    return jax.shard_map(
        shards,
        mesh=mesh,
        in_specs=(tokens, tokens, rows, rows, rows, norms, into, back, tables, tables, tables),
        out_specs=(tables, tables, rows, rows, rows, norms, into, back),
        check_vma=False,
    )
```

```python
import functools

import jax
import jax.numpy as jnp
from jax import lax
from jax.experimental import pallas as pl
from jax.experimental.pallas import tpu as pltpu
from jax.sharding import PartitionSpec as P

WIDTH = 768
HDIM = 64
SEQ = 197
ROWS = 208
EXPERTS = 16
SLOTS = 8
PLACES = EXPERTS * SLOTS
HIDDEN = 3072
EPSILON = 1e-06
SCALE = HDIM ** (-0.5)
HEADS = WIDTH // HDIM
PAIRS = HEADS // 2
HALF = 1536
EXTRA = 128
WIDE = HALF + EXTRA
BLOCK = 512
STEPS = HIDDEN // BLOCK
VMEM = 56 * 1024 * 1024
SECTION_EXPERT = ("section", "expert")

bf16 = jnp.bfloat16
f32 = jnp.float32


def mm(a, b, contract=(1, 0)):
    return lax.dot_general(
        a, b, (((contract[0],), (contract[1],)), ((), ())), preferred_element_type=f32
    )


def normalize(rows):
    centred = rows - jnp.mean(rows, axis=-1, keepdims=True)
    factor = lax.rsqrt(jnp.mean(centred * centred, axis=-1, keepdims=True) + EPSILON)
    return centred * factor, factor


def norm_backward(grad, normal, factor, gain):
    scaled = grad * gain
    inner = (
        scaled
        - jnp.mean(scaled, axis=-1, keepdims=True)
        - normal * jnp.mean(scaled * normal, axis=-1, keepdims=True)
    )
    return factor * inner


def gelu_parts(pre):
    cdf = 0.5 * (1.0 + lax.erf(pre * 0.7071067811865476))
    return cdf


def gelu_slope(pre, cdf):
    return cdf + pre * (0.3989422804014327 * jnp.exp(-0.5 * pre * pre))


def extras_of(wa_ref):
    turned = wa_ref[:, HALF:WIDE].astype(f32).T
    return turned


def selection(target_ref):
    places = lax.broadcasted_iota(jnp.int32, (PLACES, ROWS), 0)
    return (places == target_ref[0:1, :]) | (places == target_ref[1:2, :])


def slot_gates(chosen, gate_t):
    spread = jnp.broadcast_to(gate_t[:, None, :], (EXPERTS, SLOTS, ROWS)).reshape(PLACES, ROWS)
    return jnp.sum(jnp.where(chosen, spread, 0.0), axis=1, keepdims=True)


def low_lanes():
    return lax.broadcasted_iota(jnp.int32, (ROWS, 2 * HDIM), 1) < HDIM


def combine(middle, chosen, gate_t, answers):
    weighted = slot_gates(chosen, gate_t) * answers
    high = weighted.astype(bf16)
    low = (weighted - high.astype(f32)).astype(bf16)
    pick = chosen.astype(f32).astype(bf16)
    return middle + mm(pick, high, (0, 0)) + mm(pick, low, (0, 0))


def attention_forward(rows, weights, target, packed, mixed, middle_out, attend_out, gate):
    wa_ref, wb_ref = weights()
    extras = extras_of(wa_ref)
    normal, _ = normalize(rows)
    normed = (normal * extras[16:17] + extras[17:18]).astype(bf16)
    packed_ref, mixed_ref, attend_ref = packed.ref, mixed.ref, attend_out.ref
    for start in range(0, HALF, WIDTH):
        packed_ref[:, start : start + WIDTH] = mm(normed, wa_ref[:, start : start + WIDTH]).astype(
            bf16
        )
    packed_ref[:, HALF:] = mm(normed, wb_ref[:, :WIDTH]).astype(bf16)
    packed.send()
    lower = low_lanes()
    inside = lax.broadcasted_iota(jnp.int32, (ROWS, ROWS), 1) < SEQ
    for pair in range(PAIRS):
        at = pair * 128
        queries = packed_ref[:, at : at + 128]
        keys = packed_ref[:, WIDTH + at : WIDTH + at + 128]
        values = packed_ref[:, 2 * WIDTH + at : 2 * WIDTH + at + 128]
        outs = []
        for side in range(2):
            mine = lower if side == 0 else jnp.logical_not(lower)
            scores = mm(jnp.where(mine, queries, jnp.zeros_like(queries)), keys, (1, 1)) * SCALE
            scores = jnp.where(inside, scores, -1e30)
            highest = jnp.max(scores, axis=-1, keepdims=True)
            expo = jnp.exp(scores - highest)
            total = jnp.sum(expo, axis=-1, keepdims=True)
            attend = (expo * (1.0 / total)).astype(bf16)
            attend_ref[2 * pair + side] = attend
            outs.append(mm(attend, values))
        mixed_ref[:, at : at + 128] = jnp.where(lower, outs[0], outs[1]).astype(bf16)
    attend_out.send()
    mixed.send()
    middle = rows + mm(mixed_ref[...], wb_ref[:, WIDTH:HALF])
    middle_out.ref[...] = middle
    middle_out.send()
    normal, _ = normalize(middle)
    second = (normal * extras[18:19] + extras[19:20]).astype(bf16)
    logits = mm(extras[0:EXPERTS].astype(bf16), second, (1, 1))
    expo = jnp.exp(logits - jnp.max(logits, axis=0, keepdims=True))
    gate_t = expo / jnp.sum(expo, axis=0, keepdims=True)
    gate.ref[...] = gate_t
    gate.send()
    chosen = selection(target())
    buffer = mm(chosen.astype(f32).astype(bf16), second)
    return chosen, gate_t, buffer


def backward_heads(
    grad_out, answers, grad_buffer, target, gate, middle, packed, attend_in, weights,
    branch_ref, packed_grad_ref, mixed_grad_ref,
):
    gate_t = gate()[...]
    chosen = selection(target())
    pick_wide = chosen.astype(f32)
    pick = pick_wide.astype(bf16)
    arrived = mm(pick, grad_out.astype(bf16))
    grad_gates = jnp.sum(arrived * answers, axis=1, keepdims=True)
    grad_probs = jnp.sum((pick_wide * grad_gates).reshape(EXPERTS, SLOTS, ROWS), axis=1)
    grad_logits = gate_t * (grad_probs - jnp.sum(grad_probs * gate_t, axis=0, keepdims=True))
    grad_logits = grad_logits.astype(bf16)
    normal, factor = normalize(middle()[...])
    wa_ref, wb_ref = weights()
    extras = extras_of(wa_ref)
    second = (normal * extras[18:19] + extras[19:20]).astype(bf16)
    grad_router = mm(grad_logits, second)
    grad_second = mm(grad_logits, extras[0:EXPERTS].astype(bf16), (0, 0)) + mm(
        pick, grad_buffer, (0, 0)
    )
    gain_two = jnp.sum(grad_second * normal, axis=0, keepdims=True)
    shift_two = jnp.sum(grad_second, axis=0, keepdims=True)
    grad_middle = grad_out + norm_backward(grad_second, normal, factor, extras[18:19])
    branch_ref[...] = grad_middle.astype(bf16)
    mixed_grad_ref[...] = mm(branch_ref[...], wb_ref[:, WIDTH:HALF], (1, 1)).astype(bf16)
    lower = low_lanes()
    packed_ref, attend_ref = packed(), attend_in()
    for pair in range(PAIRS):
        at = pair * 128
        queries = packed_ref[:, at : at + 128]
        keys = packed_ref[:, WIDTH + at : WIDTH + at + 128]
        values = packed_ref[:, 2 * WIDTH + at : 2 * WIDTH + at + 128]
        upstream = mixed_grad_ref[:, at : at + 128]
        sums = [0.0, 0.0, 0.0]
        for side in range(2):
            mine = lower if side == 0 else jnp.logical_not(lower)
            zero = jnp.zeros_like(queries)
            upstream_one = jnp.where(mine, upstream, zero)
            attend_low = attend_ref[2 * pair + side]
            attend = attend_low.astype(f32)
            grad_attend = mm(upstream_one, values, (1, 1))
            inner = jnp.sum(grad_attend * attend, axis=-1, keepdims=True)
            grad_scores = (attend * (grad_attend - inner)).astype(bf16)
            sums[0] += mm(grad_scores, jnp.where(mine, keys, zero))
            sums[1] += mm(grad_scores, jnp.where(mine, queries, zero), (0, 0))
            sums[2] += mm(attend_low, upstream_one, (0, 0))
        packed_grad_ref[:, at : at + 128] = (sums[0] * SCALE).astype(bf16)
        packed_grad_ref[:, WIDTH + at : WIDTH + at + 128] = (sums[1] * SCALE).astype(bf16)
        packed_grad_ref[:, 2 * WIDTH + at : 2 * WIDTH + at + 128] = sums[2].astype(bf16)
    return grad_middle, extras, (grad_router, gain_two, shift_two)


def backward_rows(grad_middle, extras, small, normal_pair, weights, packed_grad_ref):
    wa_ref, wb_ref = weights()
    normal, factor = normal_pair
    grad_normed = mm(packed_grad_ref[:, :HALF], wa_ref[:, :HALF], (1, 1)) + mm(
        packed_grad_ref[:, HALF:], wb_ref[:, :WIDTH], (1, 1)
    )
    gain_one = jnp.sum(grad_normed * normal, axis=0, keepdims=True)
    shift_one = jnp.sum(grad_normed, axis=0, keepdims=True)
    grad_router, gain_two, shift_two = small
    gathered = jnp.concatenate(
        [
            grad_router,
            gain_one,
            shift_one,
            gain_two,
            shift_two,
            jnp.zeros((EXTRA - EXPERTS - 4, WIDTH), f32),
        ],
        axis=0,
    )
    return grad_middle + norm_backward(grad_normed, normal, factor, extras[16:17]), gathered


class Pair:
    def __init__(self, which, ref, mine_ref, send_ref, sems):
        self.which, self.ref, self.into, self.sems = which, ref, (mine_ref, send_ref), sems
        self.copies = []

    def put(self, half, start, value):
        at = self.which if half == 0 else 1 - self.which
        columns = slice(start, start + value.shape[1])
        self.ref[pl.ds(at, 1), :, columns] = value.astype(bf16)[None]

    def drain(self, columns):
        for at, into in enumerate(self.into):
            copy = pltpu.make_async_copy(
                self.ref.at[at, :, columns], into.at[:, columns], self.sems.at[len(self.copies)]
            )
            copy.start()
            self.copies.append(copy)

    def main(self, mixed, branch_ref, normed, packed_grad_ref):
        self.put(1, WIDTH, mm(mixed()[...], branch_ref[...], (0, 0)))
        self.put(0, 0, mm(normed, packed_grad_ref[:, 0:WIDTH], (0, 0)))
        self.put(0, WIDTH, mm(normed, packed_grad_ref[:, WIDTH:HALF], (0, 0)))
        self.put(1, 0, mm(normed, packed_grad_ref[:, HALF:], (0, 0)))
        self.drain(slice(0, HALF))

    def rest(self, gathered):
        self.put(0, HALF, gathered.T)
        self.put(1, HALF, jnp.zeros((WIDTH, EXTRA), f32))
        self.drain(slice(HALF, WIDE))

    def wait(self):
        for copy in self.copies:
            copy.wait()


def normed_rows(rows, extras):
    normal, factor = normalize(rows)
    return (normal, factor), (normal * extras[16:17] + extras[17:18]).astype(bf16)


class Arriving:
    def __init__(self, far, near, sem):
        self.copy, self.near, self.pending = pltpu.make_async_copy(far, near, sem), near, True
        self.copy.start()

    def __call__(self):
        if self.pending:
            self.copy.wait()
            self.pending = False
        return self.near


class Leaving:
    def __init__(self, far, near, sem):
        self.copy, self.ref, self.sent = pltpu.make_async_copy(near, far, sem), near, False

    def send(self):
        if not self.sent:
            self.copy.start()
            self.sent = True


class Weights:
    def __init__(self, which, own_ref, other_ref, wa_ref, wb_ref, sems):
        self.near, self.pending = (wa_ref, wb_ref), True

        @pl.when(which == 0)
        def _():
            pltpu.make_async_copy(own_ref, wa_ref, sems.at[0]).start()
            pltpu.make_async_copy(other_ref, wb_ref, sems.at[1]).start()

        @pl.when(which != 0)
        def _():
            pltpu.make_async_copy(other_ref, wa_ref, sems.at[0]).start()
            pltpu.make_async_copy(own_ref, wb_ref, sems.at[1]).start()

        self.copies = [
            pltpu.make_async_copy(own_ref, wa_ref, sems.at[0]),
            pltpu.make_async_copy(other_ref, wb_ref, sems.at[1]),
        ]

    def __call__(self):
        if self.pending:
            for copy in self.copies:
                copy.wait()
            self.pending = False
        return self.near


def first_kernel(which, weights, ins, outs, scratch):
    rows, target = ins
    send = outs[5]
    _, _, buffer = attention_forward(rows()[...].astype(f32), weights, target, *outs[:5])
    send.ref[0:PLACES] = buffer.astype(bf16)
    send.ref[PLACES:] = jnp.zeros((PLACES, WIDTH), bf16)


def second_kernel(which, weights, ins, outs, scratch):
    middle_in, gate_in, target_in, answers, grad, target = ins
    out_rows, send = outs[0], outs[6]
    out = combine(
        middle_in()[...], selection(target_in()), gate_in()[...], answers()[...].astype(f32)
    )
    out_rows.ref[...] = out.astype(bf16)
    out_rows.send()
    chosen, gate_t, buffer = attention_forward(
        out.astype(bf16).astype(f32), weights, target, *outs[1:6]
    )
    arrived = mm(chosen.astype(f32).astype(bf16), grad()[...])
    grad_answers = slot_gates(chosen, gate_t) * arrived
    both = jnp.concatenate(
        [
            buffer.reshape(EXPERTS, SLOTS, WIDTH),
            grad_answers.reshape(EXPERTS, SLOTS, WIDTH),
        ],
        axis=1,
    ).reshape(2 * PLACES, WIDTH)
    send.ref[0 : 2 * PLACES] = jnp.zeros((2 * PLACES, WIDTH), bf16)
    send.ref[2 * PLACES :] = both.astype(bf16)


def third_kernel(which, weights, ins, outs, scratch):
    back, target, gate, middle, grad, rows, packed, attend, mixed, target_next, gate_next = ins
    out_rows, grad_in_out, grad_low_out, send, mine_ref, other_grad_ref = outs
    mixed_grad_ref, packed_grad_ref, branch_ref, pair_ref, pair_sems = scratch
    pair = Pair(which, pair_ref, mine_ref, other_grad_ref, pair_sems)
    both = back()[...].astype(f32).reshape(EXPERTS, 2 * SLOTS, WIDTH)
    answers = both[:, :SLOTS].reshape(PLACES, WIDTH)
    grad_buffer = both[:, SLOTS:].reshape(PLACES, WIDTH).astype(bf16)
    out = combine(middle()[...], selection(target()), gate()[...], answers)
    out_rows.ref[...] = out.astype(bf16)
    out_rows.send()
    grad_middle, extras, small = backward_heads(
        grad()[...].astype(f32), answers, grad_buffer, target, gate, middle, packed, attend,
        weights, branch_ref, packed_grad_ref, mixed_grad_ref,
    )
    normal_pair, normed = normed_rows(rows()[...].astype(f32), extras)
    pair.main(mixed, branch_ref, normed, packed_grad_ref)
    grad_in, gathered = backward_rows(
        grad_middle, extras, small, normal_pair, weights, packed_grad_ref
    )
    pair.rest(gathered)
    grad_in_out.ref[...] = grad_in
    grad_in_out.send()
    grad_low = grad_in.astype(bf16)
    grad_low_out.ref[...] = grad_low
    grad_low_out.send()
    chosen = selection(target_next())
    arrived = mm(chosen.astype(f32).astype(bf16), grad_low)
    send.ref[0:PLACES] = (slot_gates(chosen, gate_next()[...]) * arrived).astype(bf16)
    send.ref[PLACES:] = jnp.zeros((PLACES, WIDTH), bf16)
    send.send()
    pair.wait()


def last_kernel(which, weights, ins, outs, scratch):
    target, gate, middle, grad, answers, grad_buffer, rows, packed, attend, mixed = ins
    grad_in_out, mine_ref, other_grad_ref = outs
    mixed_grad_ref, packed_grad_ref, branch_ref, pair_ref, pair_sems = scratch
    pair = Pair(which, pair_ref, mine_ref, other_grad_ref, pair_sems)
    grad_middle, extras, small = backward_heads(
        grad()[...].astype(f32), answers()[...].astype(f32), grad_buffer()[...], target, gate,
        middle, packed, attend, weights, branch_ref, packed_grad_ref, mixed_grad_ref,
    )
    normal_pair, normed = normed_rows(rows()[...].astype(f32), extras)
    pair.main(mixed, branch_ref, normed, packed_grad_ref)
    grad_in_out.ref[...], gathered = backward_rows(
        grad_middle, extras, small, normal_pair, weights, packed_grad_ref
    )
    grad_in_out.send()
    pair.rest(gathered)
    pair.wait()


def shape(*sizes, kind=bf16):
    return jax.ShapeDtypeStruct(sizes, kind)


SAVED = (
    shape(ROWS, 3 * WIDTH),
    shape(ROWS, WIDTH),
    shape(ROWS, WIDTH, kind=f32),
    shape(HEADS, ROWS, ROWS),
    shape(EXPERTS, ROWS, kind=f32),
)
WEIGHT_SCRATCH = [
    pltpu.VMEM((WIDTH, WIDE), bf16),
    pltpu.VMEM((WIDTH, WIDE), bf16),
    pltpu.SemaphoreType.DMA((2,)),
]
GRAD_SCRATCH = [
    pltpu.VMEM((ROWS, WIDTH), bf16),
    pltpu.VMEM((ROWS, 3 * WIDTH), bf16),
    pltpu.VMEM((ROWS, WIDTH), bf16),
    pltpu.VMEM((2, WIDTH, WIDE), bf16),
    pltpu.SemaphoreType.DMA((4,)),
]


def ignoring(kernel, at, count):
    def run(*refs):
        kernel(*refs[:at], *refs[at + count :])

    return run


ANYWHERE = pl.BlockSpec(memory_space=pl.ANY)


IN_HBM = pl.BlockSpec(memory_space=pltpu.HBM)


def whole(kernel, outs, scratch=(), flops=4e9, raw=0, urgent=2, earlier=()):
    def call(which, own, other, *args):
        count, made = len(args), len(outs) - raw

        def run(*refs):
            which_ref, own_ref, other_ref, *refs = refs
            far, refs = refs[:count], refs[count + len(earlier) :]
            results, refs = refs[: len(outs)], refs[len(outs) :]
            wa_ref, wb_ref, sems, in_sems, out_sems, *refs = refs
            near, refs = refs[:count], refs[count:]
            kept, rest = refs[:made], refs[made:]
            arriving = [Arriving(far[i], near[i], in_sems.at[i]) for i in range(urgent)]
            weights = Weights(which_ref[0], own_ref, other_ref, wa_ref, wb_ref, sems)
            arriving += [Arriving(far[i], near[i], in_sems.at[i]) for i in range(urgent, count)]
            leaving = [Leaving(results[i], kept[i], out_sems.at[i]) for i in range(made)]
            kernel(which_ref[0], weights, arriving, leaving + list(results[made:]), rest)
            weights()
            for each in arriving:
                each()
            for each in leaving:
                each.send()
            for each in leaving:
                each.copy.wait()

        return pl.pallas_call(
            run,
            out_shape=outs,
            in_specs=[pl.BlockSpec(memory_space=pltpu.SMEM)]
            + [IN_HBM] * (2 + count)
            + [ANYWHERE] * len(earlier),
            out_specs=(IN_HBM,) * len(outs),
            scratch_shapes=WEIGHT_SCRATCH
            + [pltpu.SemaphoreType.DMA((count,)), pltpu.SemaphoreType.DMA((max(made, 1),))]
            + [pltpu.VMEM(each.shape, each.dtype) for each in args]
            + [pltpu.VMEM(each.shape, each.dtype) for each in outs[:made]]
            + list(scratch),
            compiler_params=pltpu.CompilerParams(vmem_limit_bytes=VMEM),
            cost_estimate=pl.CostEstimate(
                flops=int(flops), bytes_accessed=12_000_000, transcendentals=600_000
            ),
        )(which, own, other, *args, *earlier)

    return call


ITEMS = 2 * EXPERTS * SLOTS


def answer_kernel(blocks, ins, outs, scratch):
    (items,), (out,), (total,) = ins, outs, scratch
    rows = items()[...]
    for step in range(STEPS):
        w_in, w_back = blocks(step)
        pre = mm(rows, w_in)
        hidden = (pre * gelu_parts(pre)).astype(bf16)
        part = mm(hidden, w_back, (1, 1))
        total[...] = part if step == 0 else total[...] + part
    out.ref[...] = total[...].astype(bf16)


def both_kernel(blocks, ins, outs, scratch):
    (mixed,), (out,), (items, grads, total, total_grad) = ins, outs, scratch
    rows = mixed()[...].astype(f32).reshape(ITEMS // SLOTS, 2 * SLOTS, WIDTH)
    items[...] = rows[:, :SLOTS].reshape(ITEMS, WIDTH).astype(bf16)
    grads[...] = rows[:, SLOTS:].reshape(ITEMS, WIDTH).astype(bf16)
    for step in range(STEPS):
        w_in, w_back = blocks(step)
        pre = mm(items[...], w_in)
        cdf = gelu_parts(pre)
        grad_hidden = mm(grads[...], w_back)
        part = mm((pre * cdf).astype(bf16), w_back, (1, 1))
        grad_pre = (grad_hidden * gelu_slope(pre, cdf)).astype(bf16)
        part_grad = mm(grad_pre, w_in, (1, 1))
        total[...] = part if step == 0 else total[...] + part
        total_grad[...] = part_grad if step == 0 else total_grad[...] + part_grad
    both = jnp.concatenate(
        [
            total[...].reshape(ITEMS // SLOTS, SLOTS, WIDTH),
            total_grad[...].reshape(ITEMS // SLOTS, SLOTS, WIDTH),
        ],
        axis=1,
    )
    out.ref[...] = both.reshape(2 * ITEMS, WIDTH).astype(bf16)


def grads_kernel(blocks, ins, outs, scratch):
    (items_in, grads_in), (out, weights_out), (total, made, sems) = ins, outs, scratch
    items, grads = items_in()[...], grads_in()[...]
    copies = []
    for step in range(STEPS):
        w_in, w_back = blocks(step)
        pre = mm(items, w_in)
        cdf = gelu_parts(pre)
        hidden = (pre * cdf).astype(bf16)
        grad_hidden = mm(grads, w_back)
        grad_pre = (grad_hidden * gelu_slope(pre, cdf)).astype(bf16)
        values = mm(items, grad_pre, (0, 0)), mm(grads, hidden, (0, 0))
        for side in range(2):
            columns = pl.ds(side * HIDDEN + step * BLOCK, BLOCK)
            made[:, columns] = values[side].astype(bf16)
            copies.append(
                pltpu.make_async_copy(
                    made.at[:, columns], weights_out.at[:, columns], sems.at[2 * step + side]
                )
            )
            copies[-1].start()
        part = mm(grad_pre, w_in, (1, 1))
        total[...] = part if step == 0 else total[...] + part
    out.ref[...] = total[...].astype(bf16)
    out.send()
    for copy in copies:
        copy.wait()


def spread_kernel(one_ref, two_ref, in_ref, out_ref):
    in_ref[...] = one_ref[...].astype(f32)
    out_ref[...] = two_ref[...].astype(f32)


def expert_outputs(total):
    rows = total.shape[0]
    block = pl.BlockSpec((rows, 2 * BLOCK), lambda j: (0, j))
    return pl.pallas_call(
        spread_kernel,
        grid=(STEPS // 2,),
        out_shape=(shape(rows, HIDDEN, kind=f32), shape(rows, HIDDEN, kind=f32)),
        in_specs=[block, pl.BlockSpec((rows, 2 * BLOCK), lambda j: (0, j + STEPS // 2))],
        out_specs=(block, block),
        cost_estimate=pl.CostEstimate(flops=0, bytes_accessed=7_000_000, transcendentals=0),
    )(total, total)


def add_kernel(mine_ref, got_ref, *out_refs):
    total = (mine_ref[...].astype(f32) + got_ref[...].astype(f32)).astype(bf16)
    start = 0
    for ref in out_refs:
        for j in range(2):
            ref[j] = total[:, j, :, start : start + ref.shape[3]]
        start += ref.shape[3]


def add_parts(mine, got, widths):
    mine, got = mine.reshape(4, 8, 24, WIDE), got.reshape(4, 8, 24, WIDE)
    block = pl.BlockSpec((4, 2, 24, WIDE), lambda j: (0, j, 0, 0))
    return pl.pallas_call(
        add_kernel,
        grid=(4,),
        out_shape=tuple(shape(8, 4, 24, width) for width in widths),
        in_specs=[block, block],
        out_specs=tuple(
            pl.BlockSpec((2, 4, 24, width), lambda j: (j, 0, 0, 0)) for width in widths
        ),
        cost_estimate=pl.CostEstimate(flops=0, bytes_accessed=8_000_000, transcendentals=0),
    )(mine, got)


def tie(array, *earlier):
    return pl.pallas_call(
        lambda *refs: None,
        out_shape=jax.ShapeDtypeStruct(array.shape, array.dtype),
        in_specs=[ANYWHERE] * (1 + len(earlier)),
        out_specs=ANYWHERE,
        input_output_aliases={0: 0},
        cost_estimate=pl.CostEstimate(flops=0, bytes_accessed=0, transcendentals=0),
    )(array, *earlier)


def place_kernel(at_ref, *refs):
    pieces, out_ref = refs[:4], refs[4]
    for number, by in enumerate((0, 1, 3, 2)):
        at = lax.rem(at_ref[0] - by + 4, 4)
        out_ref[:, pl.ds(at, 1)] = pieces[number][...][:, None]


def place(at, pieces, earlier):
    first, *sizes = pieces[0].shape
    return pl.pallas_call(
        ignoring(place_kernel, 5, len(earlier)),
        out_shape=shape(first, 4, *sizes),
        in_specs=[pl.BlockSpec(memory_space=pltpu.SMEM)]
        + [pl.BlockSpec(memory_space=pltpu.VMEM)] * 4
        + [ANYWHERE] * len(earlier),
        out_specs=pl.BlockSpec(memory_space=pltpu.VMEM),
        cost_estimate=pl.CostEstimate(flops=0, bytes_accessed=6_000_000, transcendentals=0),
    )(at, *pieces, *earlier)


def halves_kernel(which_ref, own_ref, other_ref, qkv_ref, out_ref, router_ref, norms_ref):
    def write(a_ref, b_ref):
        qkv_ref[:, :HALF] = a_ref[:, :HALF].astype(f32)
        qkv_ref[:, HALF:] = b_ref[:, :WIDTH].astype(f32)
        out_ref[...] = b_ref[:, WIDTH:HALF].astype(f32)
        extra = a_ref[:, HALF:].astype(f32).T
        router_ref[...] = extra[:EXPERTS]
        norms_ref[...] = extra[EXPERTS : EXPERTS + 4]

    @pl.when(which_ref[0] == 0)
    def _():
        write(own_ref, other_ref)

    @pl.when(which_ref[0] != 0)
    def _():
        write(other_ref, own_ref)


def halves_outputs(which, own, other, earlier):
    rows = own.shape[0]
    memories = (pltpu.SMEM, pltpu.VMEM, pltpu.VMEM)
    return pl.pallas_call(
        ignoring(halves_kernel, 3, len(earlier)),
        out_shape=(
            shape(rows, 3 * WIDTH, kind=f32),
            shape(rows, WIDTH, kind=f32),
            shape(EXPERTS, rows, kind=f32),
            shape(4, rows, kind=f32),
        ),
        in_specs=[pl.BlockSpec(memory_space=space) for space in memories]
        + [ANYWHERE] * len(earlier),
        out_specs=tuple(pl.BlockSpec(memory_space=pltpu.VMEM) for _ in range(4)),
    )(which, own, other, *earlier)


def expert_call(kernel, args, weights, outs, scratch, flops, raw=0, earlier=()):
    count, made = len(args), len(outs) - raw

    def run(*refs):
        far, refs = refs[:count], refs[count:]
        far_weights, refs = refs[0], refs[1 + len(earlier) :]
        results, refs = refs[: len(outs)], refs[len(outs) :]
        near_weights, sems, in_sems, out_sems, *refs = refs
        near, refs = refs[:count], refs[count:]
        kept, rest = refs[:made], refs[made:]
        arriving = [Arriving(far[i], near[i], in_sems.at[i]) for i in range(count)]
        parts = []
        for number in range(2 * STEPS):
            columns = pl.ds((number % 2) * HIDDEN + number // 2 * BLOCK, BLOCK)
            parts.append(
                Arriving(
                    far_weights.at[:, columns], near_weights.at[:, columns], sems.at[number]
                )
            )
        leaving = [Leaving(results[i], kept[i], out_sems.at[i]) for i in range(made)]

        def blocks(step):
            return parts[2 * step]()[...], parts[2 * step + 1]()[...]

        kernel(blocks, arriving, leaving + list(results[made:]), rest)
        for each in leaving:
            each.send()
        for each in leaving:
            each.copy.wait()

    return pl.pallas_call(
        run,
        out_shape=outs,
        in_specs=[IN_HBM] * (count + 1) + [ANYWHERE] * len(earlier),
        out_specs=(IN_HBM,) * len(outs),
        scratch_shapes=[
            pltpu.VMEM((WIDTH, 2 * HIDDEN), bf16),
            pltpu.SemaphoreType.DMA((2 * STEPS,)),
            pltpu.SemaphoreType.DMA((count,)),
            pltpu.SemaphoreType.DMA((made,)),
        ]
        + [pltpu.VMEM(each.shape, each.dtype) for each in args]
        + [pltpu.VMEM(each.shape, each.dtype) for each in outs[:made]]
        + list(scratch),
        compiler_params=pltpu.CompilerParams(vmem_limit_bytes=VMEM),
        cost_estimate=pl.CostEstimate(
            flops=int(flops), bytes_accessed=12_000_000, transcendentals=800_000
        ),
    )(*args, weights, *earlier)


TOTAL = pltpu.VMEM((ITEMS, WIDTH), f32)


def expert_answers(items, weights):
    return expert_call(
        answer_kernel, (items,), weights, (shape(ITEMS, WIDTH),), [TOTAL], 2.4e9
    )[0]


def expert_both(mixed, weights):
    rows = pltpu.VMEM((ITEMS, WIDTH), bf16)
    return expert_call(
        both_kernel, (mixed,), weights, (shape(2 * ITEMS, WIDTH),), [rows, rows, TOTAL, TOTAL], 4.8e9
    )[0]


def expert_grads(items, grads, weights, earlier):
    return expert_call(
        grads_kernel,
        (items, grads),
        weights,
        (shape(ITEMS, WIDTH), shape(WIDTH, 2 * HIDDEN)),
        [
            TOTAL,
            pltpu.VMEM((WIDTH, 2 * HIDDEN), bf16),
            pltpu.SemaphoreType.DMA((2 * STEPS,)),
        ],
        6e9,
        raw=1,
        earlier=earlier,
    )


def swap_sections(array):
    return lax.ppermute(array, "section", [(0, 1), (1, 0)])


def swap_cores(array):
    return lax.ppermute(array, "expert", [(i, i ^ 1) for i in range(EXPERTS)])


def shuffle(rows):
    return lax.all_to_all(rows, SECTION_EXPERT, split_axis=0, concat_axis=0, tiled=True)


def gather_dp(piece, me):
    out = jnp.zeros((4,) + piece.shape, piece.dtype)
    out = lax.dynamic_update_slice(out, piece[None], (me, 0, 0))
    for by in (1, 3, 2):
        out = lax.dynamic_update_slice(out, shift_dp(piece, by)[None], ((me - by) % 4, 0, 0))
    return out


def shift_dp(array, by):
    return lax.ppermute(array, "dp", [(i, (i + by) % 4) for i in range(4)])


def shift_z(array, by):
    pairs = [(i, i // 8 * 8 + (i % 8 + 2 * by) % 8) for i in range(EXPERTS)]
    return lax.ppermute(array, "expert", pairs)


SAME_CORE = [[core + 2 * i for i in range(8)] for core in (0, 1)]


def spread_parts(parts):
    return lax.all_to_all(
        parts, "expert", split_axis=0, concat_axis=0, tiled=True, axis_index_groups=SAME_CORE
    )


def shards(
    inputs, cotangent, qkv_weight, attn_out_weight, router_weight, norm_params, expert_in,
    expert_out, routes, slots, kept,
):
    first = lax.axis_index("section") == 0
    core = lax.rem(lax.axis_index("expert"), 2)
    even = core == 0
    which = core.reshape(1).astype(jnp.int32)

    def pick(zero, one):
        return jnp.where(first, zero, one)

    expert_shard = jnp.concatenate([expert_in[0, 0], expert_out[0, 0].T], axis=1)
    expert_weights = lax.all_gather(expert_shard, "dp", axis=0, tiled=True)

    extra = jnp.concatenate(
        [
            router_weight[0],
            norm_params[0].T,
            jnp.zeros((router_weight.shape[1], EXTRA - EXPERTS - 4), bf16),
        ],
        axis=1,
    )
    mine = jnp.concatenate(
        [
            jnp.where(
                even,
                qkv_weight[0][:, :HALF],
                jnp.concatenate([qkv_weight[0][:, HALF:], attn_out_weight[0]], axis=1),
            ),
            extra,
        ],
        axis=1,
    )
    dp = lax.axis_index("dp")
    z = lax.rem(lax.axis_index("expert"), 8) // 2
    mine = lax.dynamic_slice(mine, (z * 48, 0), (48, WIDE))
    theirs = swap_sections(mine)

    over_dp_one = gather_dp(pick(mine, theirs), dp)
    over_dp_two = gather_dp(pick(theirs, mine), dp)

    def gather_z(piece):
        return [piece] + [shift_z(piece, by) for by in (1, 3, 2)]

    def halves(pieces, earlier):
        at = z.reshape(1).astype(jnp.int32)
        own = place(at, pieces, earlier).reshape(WIDTH, WIDE)
        return which, own, swap_cores(own)

    weights_one = halves(gather_z(over_dp_one), (over_dp_two,))

    target = jnp.where(kept[0] > 0, routes[0] * SLOTS + slots[0], -1)
    target = jnp.pad(
        target.transpose(0, 2, 1), ((0, 0), (0, 0), (0, ROWS - SEQ)), constant_values=-1
    )
    received = swap_sections(pick(target[1], target[0]))
    own = pick(target[0], target[1])
    target_one, target_two = pick(own, received), pick(received, own)

    edge = ((0, ROWS - SEQ), (0, 0))
    rows_one = jnp.pad(pick(inputs[0], inputs[1]), edge)
    grad_two = jnp.pad(pick(cotangent[0], cotangent[1]), edge)

    packed_1, mixed_1, middle_1, attend_1, gate_1, send = whole(
        first_kernel, SAVED + (shape(2 * PLACES, WIDTH),), urgent=1
    )(*weights_one, rows_one, target_one)
    items_1 = shuffle(send.reshape(32, SLOTS, WIDTH)).reshape(ITEMS, WIDTH)
    answers = expert_answers(items_1, expert_weights)
    weights_two = halves(gather_z(over_dp_two), (items_1,))
    answers_1 = shuffle(answers.reshape(32, SLOTS, WIDTH))[:EXPERTS].reshape(PLACES, WIDTH)

    rows_two, packed_2, mixed_2, middle_2, attend_2, gate_2, send = whole(
        second_kernel, (shape(ROWS, WIDTH),) + SAVED + (shape(4 * PLACES, WIDTH),), urgent=4
    )(*weights_two, middle_1, gate_1, target_one, answers_1, grad_two, target_two)
    items_2 = shuffle(send.reshape(32, 2 * SLOTS, WIDTH))
    back = expert_both(items_2.reshape(2 * ITEMS, WIDTH), expert_weights)
    back = shuffle(back.reshape(32, 2 * SLOTS, WIDTH))[EXPERTS:].reshape(2 * PLACES, WIDTH)
    out_two, grad_in_two, grad_one, send, mine_2, other_2 = whole(
        third_kernel,
        (
            shape(ROWS, WIDTH),
            shape(ROWS, WIDTH, kind=f32),
            shape(ROWS, WIDTH),
            shape(2 * PLACES, WIDTH),
            shape(WIDTH, WIDE),
            shape(WIDTH, WIDE),
        ),
        scratch=GRAD_SCRATCH,
        flops=8e9,
        raw=2,
        urgent=5,
    )(
        *weights_two, back, target_two, gate_2, middle_2, grad_two, rows_two, packed_2, attend_2,
        mixed_2, target_one, gate_1,
    )

    def both_micros(zero, one, kind):
        zero, one = zero[:SEQ], one[:SEQ]
        got = swap_sections(pick(one, zero).astype(bf16))
        local, far = pick(zero, one).astype(kind), got.astype(kind)
        return got, jnp.stack([pick(local, far), pick(far, local)], axis=1)

    got_out, section_outputs = both_micros(rows_two, out_two, bf16)

    grads_1 = shuffle(send.reshape(32, SLOTS, WIDTH))
    items = pick(items_1.reshape(32, SLOTS, WIDTH), items_2[:, :SLOTS]).reshape(ITEMS, WIDTH)
    grads = pick(grads_1, items_2[:, SLOTS:]).reshape(ITEMS, WIDTH)
    early, late = add_parts(mine_2, swap_cores(other_2), (896, WIDE - 896))
    early = spread_parts(early)
    back, expert_pair = expert_grads(items, grads, expert_weights, (late,))
    back = tie(back, early)
    grad_buffer = shuffle(back.reshape(32, SLOTS, WIDTH))[:EXPERTS].reshape(PLACES, WIDTH)
    late = spread_parts(tie(late, grad_buffer))
    expert_sum = lax.psum_scatter(
        tie(expert_pair, grad_buffer), "dp", scatter_dimension=0, tiled=True)
    grad_in_one, mine_1, other_1 = whole(
        last_kernel,
        (shape(ROWS, WIDTH, kind=f32), shape(WIDTH, WIDE), shape(WIDTH, WIDE)),
        earlier=(got_out,),
        scratch=GRAD_SCRATCH,
        flops=8e9,
        raw=2,
        urgent=6,
    )(
        *weights_one, target_one, gate_1, middle_1, grad_one, answers_1, grad_buffer, rows_one,
        packed_1, attend_1, mixed_1,
    )

    got_grad, grad_inputs = both_micros(grad_in_one, grad_in_two, f32)
    grad_expert_in, grad_expert_out = expert_outputs(expert_sum)

    def add_eight(got):
        return jnp.sum(got.astype(f32), axis=0).astype(bf16)

    parts = add_parts(mine_1, swap_cores(tie(other_1, late)), (WIDE,))[0]
    summed_2 = jnp.concatenate([add_eight(early), add_eight(late)], axis=2)
    parts = jnp.stack([add_eight(spread_parts(parts)), summed_2])
    got = lax.all_to_all(
        parts.reshape(8, 24, WIDE), ("section", "dp"), split_axis=0, concat_axis=0, tiled=True
    )
    total = jnp.sum(got.astype(f32), axis=0).astype(bf16)
    own = lax.all_to_all(
        jnp.broadcast_to(total[None], (8, 24, WIDE)),
        "expert", split_axis=0, concat_axis=0, tiled=True, axis_index_groups=SAME_CORE,
    ).reshape(192, WIDE)
    own = tie(own, section_outputs, grad_inputs, grad_expert_in)
    other = swap_cores(own)
    grad_qkv, grad_out, grad_router, grad_norms = halves_outputs(
        which, own, other, ()
    )
    return (
        section_outputs.transpose(1, 0, 2)[None],
        grad_inputs.transpose(1, 0, 2)[None],
        grad_qkv[None],
        grad_out[None],
        grad_router.T[None],
        grad_norms[None],
        grad_expert_in[None, None],
        grad_expert_out.T[None, None],
    )


def solution(mesh):
    tokens = P(None, ("dp", "expert"), None)
    tables = P("section", None, ("dp", "expert"), None)
    rows = P("section", "dp", None)
    norms = P("section", None, "dp")
    into = P("section", "expert", "dp", None)
    back = P("section", "expert", None, "dp")
    return jax.shard_map(
        shards,
        mesh=mesh,
        in_specs=(tokens, tokens, rows, rows, rows, norms, into, back, tables, tables, tables),
        out_specs=(tables, tables, rows, rows, rows, norms, into, back),
        check_vma=False,
    )
```

```python
import functools

import jax
import jax.numpy as jnp
from jax import lax
from jax.experimental import pallas as pl
from jax.experimental.pallas import tpu as pltpu
from jax.sharding import PartitionSpec as P

WIDTH = 768
HDIM = 64
SEQ = 197
ROWS = 208
EXPERTS = 16
SLOTS = 8
PLACES = EXPERTS * SLOTS
HIDDEN = 3072
EPSILON = 1e-06
SCALE = HDIM ** (-0.5)
HEADS = WIDTH // HDIM
PAIRS = HEADS // 2
HALF = 1536
EXTRA = 128
WIDE = HALF + EXTRA
BLOCK = 1024
STEPS = HIDDEN // BLOCK
VMEM = 56 * 1024 * 1024
SECTION_EXPERT = ("section", "expert")

bf16 = jnp.bfloat16
f32 = jnp.float32


def mm(a, b, contract=(1, 0)):
    return lax.dot_general(
        a, b, (((contract[0],), (contract[1],)), ((), ())), preferred_element_type=f32
    )


def normalize(rows):
    centred = rows - jnp.mean(rows, axis=-1, keepdims=True)
    factor = lax.rsqrt(jnp.mean(centred * centred, axis=-1, keepdims=True) + EPSILON)
    return centred * factor, factor


def norm_backward(grad, normal, factor, gain):
    scaled = grad * gain
    inner = (
        scaled
        - jnp.mean(scaled, axis=-1, keepdims=True)
        - normal * jnp.mean(scaled * normal, axis=-1, keepdims=True)
    )
    return factor * inner


def gelu_parts(pre):
    cdf = 0.5 * (1.0 + lax.erf(pre * 0.7071067811865476))
    return cdf


def gelu_slope(pre, cdf):
    return cdf + pre * (0.3989422804014327 * jnp.exp(-0.5 * pre * pre))


def extras_of(weights):
    return weights("extra").astype(f32).T


def selection(target_ref):
    places = lax.broadcasted_iota(jnp.int32, (PLACES, ROWS), 0)
    return (places == target_ref[0:1, :]) | (places == target_ref[1:2, :])


def slot_gates(chosen, gate_t):
    spread = jnp.broadcast_to(gate_t[:, None, :], (EXPERTS, SLOTS, ROWS)).reshape(PLACES, ROWS)
    return jnp.sum(jnp.where(chosen, spread, 0.0), axis=1, keepdims=True)


def low_lanes():
    return lax.broadcasted_iota(jnp.int32, (ROWS, 2 * HDIM), 1) < HDIM


def combine(middle, chosen, gate_t, answers):
    weighted = slot_gates(chosen, gate_t) * answers
    high = weighted.astype(bf16)
    low = (weighted - high.astype(f32)).astype(bf16)
    pick = chosen.astype(f32).astype(bf16)
    return middle + mm(pick, high, (0, 0)) + mm(pick, low, (0, 0))


def attention_forward(rows, weights, target, packed, mixed, middle_out, attend_out, gate):
    extras = extras_of(weights)
    normal, _ = normalize(rows)
    normed = (normal * extras[16:17] + extras[17:18]).astype(bf16)
    packed_ref, mixed_ref, attend_ref = packed.ref, mixed.ref, attend_out.ref
    for number, name in enumerate("qkv"):
        columns = slice(number * WIDTH, (number + 1) * WIDTH)
        packed_ref[:, columns] = mm(normed, weights(name)).astype(bf16)
    packed.send()
    lower = low_lanes()
    inside = lax.broadcasted_iota(jnp.int32, (ROWS, ROWS), 1) < SEQ
    for pair in range(PAIRS):
        at = pair * 128
        queries = packed_ref[:, at : at + 128]
        keys = packed_ref[:, WIDTH + at : WIDTH + at + 128]
        values = packed_ref[:, 2 * WIDTH + at : 2 * WIDTH + at + 128]
        outs = []
        for side in range(2):
            mine = lower if side == 0 else jnp.logical_not(lower)
            scores = mm(jnp.where(mine, queries, jnp.zeros_like(queries)), keys, (1, 1)) * SCALE
            scores = jnp.where(inside, scores, -1e30)
            highest = jnp.max(scores, axis=-1, keepdims=True)
            expo = jnp.exp(scores - highest)
            total = jnp.sum(expo, axis=-1, keepdims=True)
            attend = (expo * (1.0 / total)).astype(bf16)
            attend_ref[2 * pair + side] = attend
            outs.append(mm(attend, values))
        mixed_ref[:, at : at + 128] = jnp.where(lower, outs[0], outs[1]).astype(bf16)
    attend_out.send()
    mixed.send()
    middle = rows + mm(mixed_ref[...], weights("out"))
    middle_out.ref[...] = middle
    middle_out.send()
    normal, _ = normalize(middle)
    second = (normal * extras[18:19] + extras[19:20]).astype(bf16)
    logits = mm(extras[0:EXPERTS].astype(bf16), second, (1, 1))
    expo = jnp.exp(logits - jnp.max(logits, axis=0, keepdims=True))
    gate_t = expo / jnp.sum(expo, axis=0, keepdims=True)
    gate.ref[...] = gate_t
    gate.send()
    chosen = selection(target())
    buffer = mm(chosen.astype(f32).astype(bf16), second)
    return chosen, gate_t, buffer


def backward_heads(
    grad_out, answers, grad_buffer, target, gate, middle, packed, attend_in, mixed, weights, pair_out,
    branch_ref, packed_grad_ref, mixed_grad_ref,
):
    gate_t = gate()[...]
    chosen = selection(target())
    pick_wide = chosen.astype(f32)
    pick = pick_wide.astype(bf16)
    arrived = mm(pick, grad_out.astype(bf16))
    grad_gates = jnp.sum(arrived * answers, axis=1, keepdims=True)
    grad_probs = jnp.sum((pick_wide * grad_gates).reshape(EXPERTS, SLOTS, ROWS), axis=1)
    grad_logits = gate_t * (grad_probs - jnp.sum(grad_probs * gate_t, axis=0, keepdims=True))
    grad_logits = grad_logits.astype(bf16)
    normal, factor = normalize(middle()[...])
    extras = extras_of(weights)
    second = (normal * extras[18:19] + extras[19:20]).astype(bf16)
    grad_router = mm(grad_logits, second)
    grad_second = mm(grad_logits, extras[0:EXPERTS].astype(bf16), (0, 0)) + mm(
        pick, grad_buffer, (0, 0)
    )
    gain_two = jnp.sum(grad_second * normal, axis=0, keepdims=True)
    shift_two = jnp.sum(grad_second, axis=0, keepdims=True)
    grad_middle = grad_out + norm_backward(grad_second, normal, factor, extras[18:19])
    branch_ref[...] = grad_middle.astype(bf16)
    mixed_grad_ref[...] = mm(branch_ref[...], weights("out"), (1, 1)).astype(bf16)
    pair_out.put(1, WIDTH, mm(mixed()[...], branch_ref[...], (0, 0)))
    lower = low_lanes()
    packed_ref, attend_ref = packed(), attend_in()
    for pair in range(PAIRS):
        at = pair * 128
        queries = packed_ref[:, at : at + 128]
        keys = packed_ref[:, WIDTH + at : WIDTH + at + 128]
        values = packed_ref[:, 2 * WIDTH + at : 2 * WIDTH + at + 128]
        upstream = mixed_grad_ref[:, at : at + 128]
        sums = [0.0, 0.0, 0.0]
        for side in range(2):
            mine = lower if side == 0 else jnp.logical_not(lower)
            zero = jnp.zeros_like(queries)
            upstream_one = jnp.where(mine, upstream, zero)
            attend_low = attend_ref[2 * pair + side]
            attend = attend_low.astype(f32)
            grad_attend = mm(upstream_one, values, (1, 1))
            inner = jnp.sum(grad_attend * attend, axis=-1, keepdims=True)
            grad_scores = (attend * (grad_attend - inner)).astype(bf16)
            sums[0] += mm(grad_scores, jnp.where(mine, keys, zero))
            sums[1] += mm(grad_scores, jnp.where(mine, queries, zero), (0, 0))
            sums[2] += mm(attend_low, upstream_one, (0, 0))
        packed_grad_ref[:, at : at + 128] = (sums[0] * SCALE).astype(bf16)
        packed_grad_ref[:, WIDTH + at : WIDTH + at + 128] = (sums[1] * SCALE).astype(bf16)
        packed_grad_ref[:, 2 * WIDTH + at : 2 * WIDTH + at + 128] = sums[2].astype(bf16)
    return grad_middle, extras, (grad_router, gain_two, shift_two)


def backward_rows(grad_middle, extras, small, normal_pair, weights, packed_grad_ref):
    normal, factor = normal_pair
    grad_normed = 0.0
    for number, name in enumerate("qkv"):
        columns = slice(number * WIDTH, (number + 1) * WIDTH)
        grad_normed += mm(packed_grad_ref[:, columns], weights(name), (1, 1))
    gain_one = jnp.sum(grad_normed * normal, axis=0, keepdims=True)
    shift_one = jnp.sum(grad_normed, axis=0, keepdims=True)
    grad_router, gain_two, shift_two = small
    gathered = jnp.concatenate(
        [
            grad_router,
            gain_one,
            shift_one,
            gain_two,
            shift_two,
            jnp.zeros((EXTRA - EXPERTS - 4, WIDTH), f32),
        ],
        axis=0,
    )
    return grad_middle + norm_backward(grad_normed, normal, factor, extras[16:17]), gathered


class Pair:
    def __init__(self, which, ref, mine_ref, send_ref, sems):
        self.which, self.ref, self.sems = which, ref, sems
        self.mine_ref, self.send_ref = mine_ref, send_ref
        self.copies = []

    def put(self, half, start, value):
        columns = slice(start, start + value.shape[1])
        self.ref[half, :, columns] = value.astype(bf16)
        near, sem = self.ref.at[half, :, columns], self.sems.at[len(self.copies)]
        mine = pltpu.make_async_copy(near, self.mine_ref.at[:, columns], sem)
        send = pltpu.make_async_copy(near, self.send_ref.at[:, columns], sem)
        pl.when(self.which == half)(mine.start)
        pl.when(self.which != half)(send.start)
        self.copies.append(mine)

    def main(self, normed, packed_grad_ref):
        self.put(0, 0, mm(normed, packed_grad_ref[:, 0:WIDTH], (0, 0)))
        self.put(0, WIDTH, mm(normed, packed_grad_ref[:, WIDTH:HALF], (0, 0)))
        self.put(1, 0, mm(normed, packed_grad_ref[:, HALF:], (0, 0)))

    def rest(self, gathered):
        self.put(0, HALF, gathered.T)
        self.put(1, HALF, jnp.zeros((WIDTH, EXTRA), f32))

    def wait(self):
        for copy in self.copies:
            copy.wait()


def normed_rows(rows, extras):
    normal, factor = normalize(rows)
    return (normal, factor), (normal * extras[16:17] + extras[17:18]).astype(bf16)


class Arriving:
    def __init__(self, far, near, sem):
        self.copy, self.near, self.pending = pltpu.make_async_copy(far, near, sem), near, True
        self.copy.start()

    def __call__(self):
        if self.pending:
            self.copy.wait()
            self.pending = False
        return self.near


class Leaving:
    def __init__(self, far, near, sem):
        self.copy, self.ref, self.sent = pltpu.make_async_copy(near, far, sem), near, False

    def send(self):
        if not self.sent:
            self.copy.start()
            self.sent = True


CHUNKS = {
    "q": (0, 0, WIDTH),
    "k": (0, WIDTH, WIDTH),
    "extra": (0, HALF, EXTRA),
    "v": (1, 0, WIDTH),
    "out": (1, WIDTH, WIDTH),
}


class Weights:
    def __init__(self, which, own_ref, other_ref, near_ref, sems):
        self.near, self.pending, self.copies = near_ref, [0, 1], []
        for half in range(2):
            copies = [
                pltpu.make_async_copy(source, near_ref.at[half], sems.at[half])
                for source in (own_ref, other_ref)
            ]
            pl.when(which == half)(copies[0].start)
            pl.when(which != half)(copies[1].start)
            self.copies.append(copies[0])

    def __call__(self, name):
        half, start, width = CHUNKS[name]
        if half in self.pending:
            self.copies[half].wait()
            self.pending.remove(half)
        return self.near[half, :, start : start + width]


def first_kernel(which, weights, ins, outs, scratch):
    rows, target = ins
    send = outs[5]
    _, _, buffer = attention_forward(rows()[...].astype(f32), weights, target, *outs[:5])
    send.ref[0:PLACES] = buffer.astype(bf16)
    send.ref[PLACES:] = jnp.zeros((PLACES, WIDTH), bf16)


def second_kernel(which, weights, ins, outs, scratch):
    middle_in, gate_in, target_in, answers, grad, target = ins
    out_rows, send = outs[0], outs[6]
    out = combine(
        middle_in()[...], selection(target_in()), gate_in()[...], answers()[...].astype(f32)
    )
    out_rows.ref[...] = out.astype(bf16)
    out_rows.send()
    chosen, gate_t, buffer = attention_forward(
        out.astype(bf16).astype(f32), weights, target, *outs[1:6]
    )
    arrived = mm(chosen.astype(f32).astype(bf16), grad()[...])
    grad_answers = slot_gates(chosen, gate_t) * arrived
    both = jnp.concatenate(
        [
            buffer.reshape(EXPERTS, SLOTS, WIDTH),
            grad_answers.reshape(EXPERTS, SLOTS, WIDTH),
        ],
        axis=1,
    ).reshape(2 * PLACES, WIDTH)
    send.ref[0 : 2 * PLACES] = jnp.zeros((2 * PLACES, WIDTH), bf16)
    send.ref[2 * PLACES :] = both.astype(bf16)


def third_kernel(which, weights, ins, outs, scratch):
    back, target, gate, middle, grad, rows, packed, attend, mixed, target_next, gate_next = ins
    out_rows, grad_in_out, grad_low_out, send, mine_ref, other_grad_ref = outs
    mixed_grad_ref, packed_grad_ref, branch_ref, pair_ref, pair_sems = scratch
    pair = Pair(which, pair_ref, mine_ref, other_grad_ref, pair_sems)
    both = back()[...].astype(f32).reshape(EXPERTS, 2 * SLOTS, WIDTH)
    answers = both[:, :SLOTS].reshape(PLACES, WIDTH)
    grad_buffer = both[:, SLOTS:].reshape(PLACES, WIDTH).astype(bf16)
    out = combine(middle()[...], selection(target()), gate()[...], answers)
    out_rows.ref[...] = out.astype(bf16)
    out_rows.send()
    grad_middle, extras, small = backward_heads(
        grad()[...].astype(f32), answers, grad_buffer, target, gate, middle, packed, attend,
        mixed, weights, pair, branch_ref, packed_grad_ref, mixed_grad_ref,
    )
    normal_pair, normed = normed_rows(rows()[...].astype(f32), extras)
    pair.main(normed, packed_grad_ref)
    grad_in, gathered = backward_rows(
        grad_middle, extras, small, normal_pair, weights, packed_grad_ref
    )
    pair.rest(gathered)
    grad_in_out.ref[...] = grad_in
    grad_in_out.send()
    grad_low = grad_in.astype(bf16)
    grad_low_out.ref[...] = grad_low
    grad_low_out.send()
    chosen = selection(target_next())
    arrived = mm(chosen.astype(f32).astype(bf16), grad_low)
    send.ref[0:PLACES] = (slot_gates(chosen, gate_next()[...]) * arrived).astype(bf16)
    send.ref[PLACES:] = jnp.zeros((PLACES, WIDTH), bf16)
    send.send()
    pair.wait()


def last_kernel(which, weights, ins, outs, scratch):
    target, gate, middle, grad, answers, grad_buffer, rows, packed, attend, mixed = ins
    grad_in_out, mine_ref, other_grad_ref = outs
    mixed_grad_ref, packed_grad_ref, branch_ref, pair_ref, pair_sems = scratch
    pair = Pair(which, pair_ref, mine_ref, other_grad_ref, pair_sems)
    grad_middle, extras, small = backward_heads(
        grad()[...].astype(f32), answers()[...].astype(f32), grad_buffer()[...], target, gate,
        middle, packed, attend, mixed, weights, pair, branch_ref, packed_grad_ref, mixed_grad_ref,
    )
    normal_pair, normed = normed_rows(rows()[...].astype(f32), extras)
    pair.main(normed, packed_grad_ref)
    grad_in_out.ref[...], gathered = backward_rows(
        grad_middle, extras, small, normal_pair, weights, packed_grad_ref
    )
    grad_in_out.send()
    pair.rest(gathered)
    pair.wait()


def shape(*sizes, kind=bf16):
    return jax.ShapeDtypeStruct(sizes, kind)


SAVED = (
    shape(ROWS, 3 * WIDTH),
    shape(ROWS, WIDTH),
    shape(ROWS, WIDTH, kind=f32),
    shape(HEADS, ROWS, ROWS),
    shape(EXPERTS, ROWS, kind=f32),
)
WEIGHT_SCRATCH = [
    pltpu.VMEM((2, WIDTH, WIDE), bf16),
    pltpu.SemaphoreType.DMA((2,)),
]
GRAD_SCRATCH = [
    pltpu.VMEM((ROWS, WIDTH), bf16),
    pltpu.VMEM((ROWS, 3 * WIDTH), bf16),
    pltpu.VMEM((ROWS, WIDTH), bf16),
    pltpu.VMEM((2, WIDTH, WIDE), bf16),
    pltpu.SemaphoreType.DMA((6,)),
]


def ignoring(kernel, at, count):
    def run(*refs):
        kernel(*refs[:at], *refs[at + count :])

    return run


ANYWHERE = pl.BlockSpec(memory_space=pl.ANY)


IN_HBM = pl.BlockSpec(memory_space=pltpu.HBM)


def part(array, start, rows):
    return array, start, rows


def operands(args):
    parts = [each if isinstance(each, tuple) else (each, 0, each.shape[0]) for each in args]
    arrays = [array for array, _, _ in parts]
    slices = [pl.ds(start, rows) for _, start, rows in parts]
    scratch = [
        pltpu.VMEM((rows,) + array.shape[1:], array.dtype) for array, _, rows in parts
    ]
    return arrays, slices, scratch


def whole(kernel, outs, scratch=(), flops=4e9, raw=0, urgent=2, earlier=()):
    def call(which, own, other, *args):
        count, made = len(args), len(outs) - raw
        arrays, slices, buffers = operands(args)

        def run(*refs):
            which_ref, own_ref, other_ref, *refs = refs
            far, refs = refs[:count], refs[count + len(earlier) :]
            results, refs = refs[: len(outs)], refs[len(outs) :]
            weights_ref, sems, in_sems, out_sems, *refs = refs
            near, refs = refs[:count], refs[count:]
            kept, rest = refs[:made], refs[made:]

            def arrive(places):
                return [Arriving(far[i].at[slices[i]], near[i], in_sems.at[i]) for i in places]

            arriving = arrive(range(urgent))
            weights = Weights(which_ref[0], own_ref, other_ref, weights_ref, sems)
            arriving += arrive(range(urgent, count))
            leaving = [Leaving(results[i], kept[i], out_sems.at[i]) for i in range(made)]
            kernel(which_ref[0], weights, arriving, leaving + list(results[made:]), rest)
            for each in leaving:
                each.send()
            for each in leaving:
                each.copy.wait()

        return pl.pallas_call(
            run,
            out_shape=outs,
            in_specs=[pl.BlockSpec(memory_space=pltpu.SMEM)]
            + [IN_HBM] * (2 + count)
            + [ANYWHERE] * len(earlier),
            out_specs=(IN_HBM,) * len(outs),
            scratch_shapes=WEIGHT_SCRATCH
            + [pltpu.SemaphoreType.DMA((count,)), pltpu.SemaphoreType.DMA((max(made, 1),))]
            + buffers
            + [pltpu.VMEM(each.shape, each.dtype) for each in outs[:made]]
            + list(scratch),
            compiler_params=pltpu.CompilerParams(vmem_limit_bytes=VMEM),
            cost_estimate=pl.CostEstimate(
                flops=int(flops), bytes_accessed=12_000_000, transcendentals=600_000
            ),
        )(which, own, other, *arrays, *earlier)

    return call


ITEMS = 2 * EXPERTS * SLOTS


def answer_kernel(blocks, ins, outs, scratch):
    (items,), (out,), (total,) = ins, outs, scratch
    rows = items()[...]
    for step in range(STEPS):
        w_in, w_back = blocks(step)
        pre = mm(rows, w_in)
        hidden = (pre * gelu_parts(pre)).astype(bf16)
        part = mm(hidden, w_back, (1, 1))
        total[...] = part if step == 0 else total[...] + part
    out.ref[...] = total[...].astype(bf16)


def both_kernel(blocks, ins, outs, scratch):
    (mixed,), (out,), (items, grads, total, total_grad) = ins, outs, scratch
    rows = mixed()[...].astype(f32).reshape(ITEMS // SLOTS, 2 * SLOTS, WIDTH)
    items[...] = rows[:, :SLOTS].reshape(ITEMS, WIDTH).astype(bf16)
    grads[...] = rows[:, SLOTS:].reshape(ITEMS, WIDTH).astype(bf16)
    for step in range(STEPS):
        w_in, w_back = blocks(step)
        pre = mm(items[...], w_in)
        cdf = gelu_parts(pre)
        grad_hidden = mm(grads[...], w_back)
        part = mm((pre * cdf).astype(bf16), w_back, (1, 1))
        grad_pre = (grad_hidden * gelu_slope(pre, cdf)).astype(bf16)
        part_grad = mm(grad_pre, w_in, (1, 1))
        total[...] = part if step == 0 else total[...] + part
        total_grad[...] = part_grad if step == 0 else total_grad[...] + part_grad
    both = jnp.concatenate(
        [
            total[...].reshape(ITEMS // SLOTS, SLOTS, WIDTH),
            total_grad[...].reshape(ITEMS // SLOTS, SLOTS, WIDTH),
        ],
        axis=1,
    )
    out.ref[...] = both.reshape(2 * ITEMS, WIDTH).astype(bf16)


def grads_kernel(blocks, ins, outs, scratch):
    (items, grads), (out,), (total,) = ins, outs, scratch
    rows, grad_rows = items()[...], grads()[...]
    for step in range(STEPS):
        w_in, w_back = blocks(step)
        pre = mm(rows, w_in)
        grad_hidden = mm(grad_rows, w_back)
        grad_pre = (grad_hidden * gelu_slope(pre, gelu_parts(pre))).astype(bf16)
        part = mm(grad_pre, w_in, (1, 1))
        total[...] = part if step == 0 else total[...] + part
    out.ref[...] = total[...].astype(bf16)


SLICE = HIDDEN // 4
GROUP = 256


def slice_kernel(
    dp_ref, rows_ref, w_ref, *refs
):
    outs, refs = refs[:4], refs[4:]
    rows_near, w_near, items, grads, turned, made, sems, out_sems = refs
    at = dp_ref[0]
    arriving = [
        Arriving(
            w_ref.at[:, pl.ds(pl.multiple_of(side * HIDDEN + at * SLICE, 128), SLICE)],
            w_near.at[side],
            sems.at[side],
        )
        for side in range(2)
    ]
    blocks = [
        Arriving(rows_ref.at[pl.ds(i * 2 * ITEMS, 2 * ITEMS)], rows_near.at[i], sems.at[2 + i])
        for i in range(4)
    ]
    for i in range(4):
        rows = blocks[i]()[...].astype(f32).reshape(ITEMS // SLOTS, 2 * SLOTS, WIDTH)
        place = slice(i * ITEMS, (i + 1) * ITEMS)
        for side, into in enumerate((items, grads)):
            mine = rows[:, side * SLOTS : (side + 1) * SLOTS].reshape(ITEMS, WIDTH).astype(bf16)
            into[place] = mine
            turned[side, :, place] = mine.T
    w_in, w_back = arriving[0](), arriving[1]()
    for start in range(0, SLICE, GROUP):
        columns = slice(start, start + GROUP)
        pre = mm(items[...], w_in[:, columns])
        cdf = gelu_parts(pre)
        grad_hidden = mm(grads[...], w_back[:, columns])
        grad_pre = (grad_hidden * gelu_slope(pre, cdf)).astype(bf16)
        hidden = (pre * cdf).astype(bf16)
        made[:, columns] = mm(turned[0], grad_pre).astype(bf16)
        made[:, SLICE + start : SLICE + start + GROUP] = mm(turned[1], hidden).astype(bf16)
    copies = []
    for by in range(4):
        rows = pl.ds(pl.multiple_of(lax.rem(at + by, 4) * 192, 16), 192)
        copies.append(pltpu.make_async_copy(made.at[rows], outs[by], out_sems.at[by]))
        copies[-1].start()
    for copy in copies:
        copy.wait()


def slice_grads(dp, rows, weights, earlier):
    return pl.pallas_call(
        ignoring(slice_kernel, 3, len(earlier)),
        out_shape=(shape(192, 2 * SLICE),) * 4,
        in_specs=[pl.BlockSpec(memory_space=pltpu.SMEM)]
        + [IN_HBM] * 2
        + [ANYWHERE] * len(earlier),
        out_specs=(IN_HBM,) * 4,
        scratch_shapes=[
            pltpu.VMEM((4, 2 * ITEMS, WIDTH), bf16),
            pltpu.VMEM((2, WIDTH, SLICE), bf16),
            pltpu.VMEM((4 * ITEMS, WIDTH), bf16),
            pltpu.VMEM((4 * ITEMS, WIDTH), bf16),
            pltpu.VMEM((2, WIDTH, 4 * ITEMS), bf16),
            pltpu.VMEM((WIDTH, 2 * SLICE), bf16),
            pltpu.SemaphoreType.DMA((6,)),
            pltpu.SemaphoreType.DMA((4,)),
        ],
        compiler_params=pltpu.CompilerParams(vmem_limit_bytes=VMEM),
        cost_estimate=pl.CostEstimate(
            flops=5_000_000_000, bytes_accessed=9_000_000, transcendentals=800_000
        ),
    )(dp, rows, weights, *earlier)


def spread_kernel(dp_ref, *refs):
    pieces, (in_ref, out_ref) = refs[:4], refs[4:]
    for by, ref in enumerate(pieces):
        at = lax.rem(dp_ref[0] - by + 4, 4)
        columns = pl.ds(pl.multiple_of(at * SLICE, 128), SLICE)
        in_ref[:, columns] = ref[:, :SLICE].astype(f32)
        out_ref[:, columns] = ref[:, SLICE:].astype(f32)


def expert_outputs(dp, pieces):
    return pl.pallas_call(
        spread_kernel,
        out_shape=(shape(192, HIDDEN, kind=f32), shape(192, HIDDEN, kind=f32)),
        in_specs=[pl.BlockSpec(memory_space=pltpu.SMEM)]
        + [pl.BlockSpec(memory_space=pltpu.VMEM)] * 4,
        out_specs=(pl.BlockSpec(memory_space=pltpu.VMEM),) * 2,
        compiler_params=pltpu.CompilerParams(vmem_limit_bytes=VMEM),
        cost_estimate=pl.CostEstimate(flops=0, bytes_accessed=7_000_000, transcendentals=0),
    )(dp, *pieces)


def add_parts(mine, got, widths):
    def run(mine_ref, got_ref, *refs):
        results, refs = refs[: len(widths)], refs[len(widths) :]
        mine_near, got_near, in_sems, out_sems, *made = refs
        arriving = [
            [
                Arriving(far.at[:, j], near.at[j], in_sems.at[2 * j + side])
                for side, (far, near) in enumerate(((mine_ref, mine_near), (got_ref, got_near)))
            ]
            for j in range(8)
        ]
        copies = []
        for j in range(8):
            one, two = [each()[...].astype(f32) for each in arriving[j]]
            total = (one + two).astype(bf16)
            start = 0
            for number, width in enumerate(widths):
                made[number][j] = total[:, :, start : start + width]
                copies.append(
                    pltpu.make_async_copy(
                        made[number].at[j], results[number].at[j], out_sems.at[len(copies)]
                    )
                )
                copies[-1].start()
                start += width
        for copy in copies:
            copy.wait()

    return pl.pallas_call(
        run,
        out_shape=tuple(shape(8, 4, 24, width) for width in widths),
        in_specs=[ANYWHERE] * 2,
        out_specs=(IN_HBM,) * len(widths),
        scratch_shapes=[
            pltpu.VMEM((8, 4, 24, WIDE), bf16),
            pltpu.VMEM((8, 4, 24, WIDE), bf16),
            pltpu.SemaphoreType.DMA((16,)),
            pltpu.SemaphoreType.DMA((8 * len(widths),)),
        ]
        + [pltpu.VMEM((8, 4, 24, width), bf16) for width in widths],
        compiler_params=pltpu.CompilerParams(vmem_limit_bytes=VMEM),
        cost_estimate=pl.CostEstimate(flops=0, bytes_accessed=8_000_000, transcendentals=0),
    )(mine.reshape(4, 8, 24, WIDE), got.reshape(4, 8, 24, WIDE))


def tie(array, *earlier):
    return pl.pallas_call(
        lambda *refs: None,
        out_shape=jax.ShapeDtypeStruct(array.shape, array.dtype),
        in_specs=[IN_HBM] + [ANYWHERE] * len(earlier),
        out_specs=IN_HBM,
        input_output_aliases={0: 0},
        cost_estimate=pl.CostEstimate(flops=0, bytes_accessed=0, transcendentals=0),
    )(array, *earlier)


def place_kernel(at_ref, *refs):
    pieces, out_ref = refs[:4], refs[4]
    for number, by in enumerate((0, 1, 3, 2)):
        at = lax.rem(at_ref[0] - by + 4, 4)
        out_ref[:, pl.ds(at, 1)] = pieces[number][...][:, None]


def place(at, pieces, earlier):
    first, *sizes = pieces[0].shape
    return pl.pallas_call(
        ignoring(place_kernel, 5, len(earlier)),
        out_shape=shape(first, 4, *sizes),
        in_specs=[pl.BlockSpec(memory_space=pltpu.SMEM)]
        + [pl.BlockSpec(memory_space=pltpu.VMEM)] * 4
        + [ANYWHERE] * len(earlier),
        out_specs=pl.BlockSpec(memory_space=pltpu.VMEM),
        cost_estimate=pl.CostEstimate(flops=0, bytes_accessed=6_000_000, transcendentals=0),
    )(at, *pieces, *earlier)


def halves_kernel(which_ref, own_ref, other_ref, qkv_ref, out_ref, router_ref, norms_ref):
    def write(a_ref, b_ref):
        qkv_ref[:, :HALF] = a_ref[:, :HALF].astype(f32)
        qkv_ref[:, HALF:] = b_ref[:, :WIDTH].astype(f32)
        out_ref[...] = b_ref[:, WIDTH:HALF].astype(f32)
        extra = a_ref[:, HALF:].astype(f32).T
        router_ref[...] = extra[:EXPERTS]
        norms_ref[...] = extra[EXPERTS : EXPERTS + 4]

    @pl.when(which_ref[0] == 0)
    def _():
        write(own_ref, other_ref)

    @pl.when(which_ref[0] != 0)
    def _():
        write(other_ref, own_ref)


def halves_outputs(which, own, other, earlier):
    rows = own.shape[0]
    memories = (pltpu.SMEM, pltpu.VMEM, pltpu.VMEM)
    return pl.pallas_call(
        ignoring(halves_kernel, 3, len(earlier)),
        out_shape=(
            shape(rows, 3 * WIDTH, kind=f32),
            shape(rows, WIDTH, kind=f32),
            shape(EXPERTS, rows, kind=f32),
            shape(4, rows, kind=f32),
        ),
        in_specs=[pl.BlockSpec(memory_space=space) for space in memories]
        + [ANYWHERE] * len(earlier),
        out_specs=tuple(pl.BlockSpec(memory_space=pltpu.VMEM) for _ in range(4)),
    )(which, own, other, *earlier)


def stack_kernel(flag_ref, zero_ref, one_ref, got_ref, out_ref):
    @pl.when(flag_ref[0] == 0)
    def _():
        out_ref[:, 0, :] = zero_ref[0:SEQ, :]
        out_ref[:, 1, :] = got_ref[...].astype(f32)

    @pl.when(flag_ref[0] != 0)
    def _():
        out_ref[:, 0, :] = got_ref[...].astype(f32)
        out_ref[:, 1, :] = one_ref[0:SEQ, :]


def stack_micros(flag, zero, one, got):
    memories = (pltpu.SMEM, pltpu.VMEM, pltpu.VMEM, pltpu.VMEM)
    return pl.pallas_call(
        stack_kernel,
        out_shape=shape(SEQ, 2, WIDTH, kind=f32),
        in_specs=[pl.BlockSpec(memory_space=space) for space in memories],
        out_specs=pl.BlockSpec(memory_space=pltpu.VMEM),
        cost_estimate=pl.CostEstimate(flops=0, bytes_accessed=3_000_000, transcendentals=0),
    )(flag, zero, one, got)


def expert_call(kernel, args, weights, outs, scratch, flops, raw=0, earlier=(), flags=()):
    count, made = len(args), len(outs) - raw

    def run(*refs):
        scalars, refs = [ref[0] for ref in refs[: len(flags)]], refs[len(flags) :]
        far, refs = refs[:count], refs[count:]
        far_weights, refs = refs[0], refs[1 + len(earlier) :]
        results, refs = refs[: len(outs)], refs[len(outs) :]
        near_weights, sems, in_sems, out_sems, *refs = refs
        near, refs = refs[:count], refs[count:]
        kept, rest = refs[:made], refs[made:]
        arriving = [Arriving(far[i], near[i], in_sems.at[i]) for i in range(count)]
        parts = []
        for number in range(2 * STEPS):
            columns = pl.ds((number % 2) * HIDDEN + number // 2 * BLOCK, BLOCK)
            parts.append(
                Arriving(
                    far_weights.at[:, columns], near_weights.at[:, columns], sems.at[number]
                )
            )
        leaving = [Leaving(results[i], kept[i], out_sems.at[i]) for i in range(made)]

        def blocks(step):
            return parts[2 * step]()[...], parts[2 * step + 1]()[...]

        kernel(blocks, scalars + arriving, leaving + list(results[made:]), rest)
        for each in leaving:
            each.send()
        for each in leaving:
            each.copy.wait()

    return pl.pallas_call(
        run,
        out_shape=outs,
        in_specs=[pl.BlockSpec(memory_space=pltpu.SMEM)] * len(flags)
        + [IN_HBM] * (count + 1)
        + [ANYWHERE] * len(earlier),
        out_specs=(IN_HBM,) * len(outs),
        scratch_shapes=[
            pltpu.VMEM((WIDTH, 2 * HIDDEN), bf16),
            pltpu.SemaphoreType.DMA((2 * STEPS,)),
            pltpu.SemaphoreType.DMA((count,)),
            pltpu.SemaphoreType.DMA((made,)),
        ]
        + [pltpu.VMEM(each.shape, each.dtype) for each in args]
        + [pltpu.VMEM(each.shape, each.dtype) for each in outs[:made]]
        + list(scratch),
        compiler_params=pltpu.CompilerParams(vmem_limit_bytes=VMEM),
        cost_estimate=pl.CostEstimate(
            flops=int(flops), bytes_accessed=12_000_000, transcendentals=800_000
        ),
    )(*flags, *args, weights, *earlier)


TOTAL = pltpu.VMEM((ITEMS, WIDTH), f32)


def expert_answers(items, weights):
    return expert_call(
        answer_kernel, (items,), weights, (shape(ITEMS, WIDTH),), [TOTAL], 2.4e9
    )[0]


def expert_both(mixed, weights):
    rows = pltpu.VMEM((ITEMS, WIDTH), bf16)
    return expert_call(
        both_kernel, (mixed,), weights, (shape(2 * ITEMS, WIDTH),), [rows, rows, TOTAL, TOTAL], 4.8e9
    )[0]


def expert_grads(items, grads, weights):
    return expert_call(
        grads_kernel, (items, grads), weights, (shape(ITEMS, WIDTH),), [TOTAL], 3.6e9
    )[0]


def swap_sections(array):
    return lax.ppermute(array, "section", [(0, 1), (1, 0)])


def swap_cores(array):
    return lax.ppermute(array, "expert", [(i, i ^ 1) for i in range(EXPERTS)])


def shuffle(rows):
    return lax.all_to_all(rows, SECTION_EXPERT, split_axis=0, concat_axis=0, tiled=True)


def gather_dp(piece, me):
    out = jnp.zeros((4,) + piece.shape, piece.dtype)
    out = lax.dynamic_update_slice(out, piece[None], (me, 0, 0))
    for by in (1, 3, 2):
        out = lax.dynamic_update_slice(out, shift_dp(piece, by)[None], ((me - by) % 4, 0, 0))
    return out


def shift_dp(array, by):
    return lax.ppermute(array, "dp", [(i, (i + by) % 4) for i in range(4)])


def shift_z(array, by):
    pairs = [(i, i // 8 * 8 + (i % 8 + 2 * by) % 8) for i in range(EXPERTS)]
    return lax.ppermute(array, "expert", pairs)


SAME_CORE = [[core + 2 * i for i in range(8)] for core in (0, 1)]


def spread_parts(parts):
    return lax.all_to_all(
        parts, "expert", split_axis=0, concat_axis=0, tiled=True, axis_index_groups=SAME_CORE
    )


def shards(
    inputs, cotangent, qkv_weight, attn_out_weight, router_weight, norm_params, expert_in,
    expert_out, routes, slots, kept,
):
    section = lax.axis_index("section")
    first = section == 0
    core = lax.rem(lax.axis_index("expert"), 2)
    even = core == 0
    which = core.reshape(1).astype(jnp.int32)

    def pick(zero, one):
        return jnp.where(first, zero, one)

    expert_shard = jnp.concatenate([expert_in[0, 0], expert_out[0, 0].T], axis=1)
    expert_weights = lax.all_gather(expert_shard, "dp", axis=0, tiled=True)

    extra = jnp.concatenate(
        [
            router_weight[0],
            norm_params[0].T,
            jnp.zeros((router_weight.shape[1], EXTRA - EXPERTS - 4), bf16),
        ],
        axis=1,
    )
    mine = jnp.concatenate(
        [
            jnp.where(
                even,
                qkv_weight[0][:, :HALF],
                jnp.concatenate([qkv_weight[0][:, HALF:], attn_out_weight[0]], axis=1),
            ),
            extra,
        ],
        axis=1,
    )
    dp = lax.axis_index("dp")
    z = lax.rem(lax.axis_index("expert"), 8) // 2
    mine = lax.dynamic_slice(mine, (z * 48, 0), (48, WIDE))
    theirs = swap_sections(mine)

    over_dp_one = gather_dp(pick(mine, theirs), dp)
    over_dp_two = gather_dp(pick(theirs, mine), dp)

    def gather_z(piece):
        return [piece] + [shift_z(piece, by) for by in (1, 3, 2)]

    def halves(pieces, earlier):
        at = z.reshape(1).astype(jnp.int32)
        own = place(at, pieces, earlier).reshape(WIDTH, WIDE)
        return which, own, swap_cores(own)

    weights_one = halves(gather_z(over_dp_one), (over_dp_two,))

    target = jnp.where(kept[0] > 0, routes[0] * SLOTS + slots[0], -1)
    target = jnp.pad(
        target.transpose(0, 2, 1), ((0, 0), (0, 0), (0, ROWS - SEQ)), constant_values=-1
    )
    received = swap_sections(pick(target[1], target[0]))
    own = pick(target[0], target[1])
    target_one, target_two = pick(own, received), pick(received, own)

    edge = ((0, ROWS - SEQ), (0, 0))
    rows_one = jnp.pad(pick(inputs[0], inputs[1]), edge)
    grad_two = jnp.pad(pick(cotangent[0], cotangent[1]), edge)

    packed_1, mixed_1, middle_1, attend_1, gate_1, send = whole(
        first_kernel, SAVED + (shape(2 * PLACES, WIDTH),), urgent=1
    )(*weights_one, rows_one, target_one)
    items_1 = shuffle(send.reshape(32, SLOTS, WIDTH)).reshape(ITEMS, WIDTH)
    answers = expert_answers(items_1, expert_weights)
    weights_two = halves(gather_z(over_dp_two), (items_1,))
    answers_1 = shuffle(answers.reshape(32, SLOTS, WIDTH)).reshape(ITEMS, WIDTH)
    answers_1 = part(answers_1, 0, PLACES)

    rows_two, packed_2, mixed_2, middle_2, attend_2, gate_2, send = whole(
        second_kernel,
        (shape(ROWS, WIDTH),) + SAVED + (shape(4 * PLACES, WIDTH),),
        urgent=4,
    )(*weights_two, middle_1, gate_1, target_one, answers_1, grad_two, target_two)
    items_2 = shuffle(send.reshape(32, 2 * SLOTS, WIDTH)).reshape(2 * ITEMS, WIDTH)
    back = expert_both(items_2, expert_weights)
    back = shuffle(back.reshape(32, 2 * SLOTS, WIDTH)).reshape(2 * ITEMS, WIDTH)
    back = part(back, 2 * PLACES, 2 * PLACES)
    out_two, grad_in_two, grad_one, send, mine_2, other_2 = whole(
        third_kernel,
        (
            shape(ROWS, WIDTH),
            shape(ROWS, WIDTH, kind=f32),
            shape(ROWS, WIDTH),
            shape(2 * PLACES, WIDTH),
            shape(WIDTH, WIDE),
            shape(WIDTH, WIDE),
        ),
        scratch=GRAD_SCRATCH,
        flops=8e9,
        raw=2,
        urgent=5,
    )(
        *weights_two, back, target_two, gate_2, middle_2, grad_two, rows_two, packed_2, attend_2,
        mixed_2, target_one, gate_1,
    )

    got_out = swap_sections(pick(out_two, rows_two)[:SEQ])
    own_out = pick(rows_two, out_two)[:SEQ]
    section_outputs = jnp.stack([pick(own_out, got_out), pick(got_out, own_out)], axis=1)

    grads_1 = shuffle(send.reshape(32, SLOTS, WIDTH)).reshape(ITEMS, WIDTH)
    parts_2 = add_parts(mine_2, swap_cores(other_2), (WIDE,))[0]
    back = expert_grads(items_1, grads_1, expert_weights)
    grad_buffer = shuffle(back.reshape(32, SLOTS, WIDTH)).reshape(ITEMS, WIDTH)
    mixed_one = jnp.concatenate(
        [items_1.reshape(32, SLOTS, WIDTH), grads_1.reshape(32, SLOTS, WIDTH)], axis=1
    )
    expert_rows = lax.all_gather(
        pick(mixed_one.reshape(2 * ITEMS, WIDTH), items_2), "dp", axis=0, tiled=True
    )
    summed_2 = lax.psum_scatter(
        tie(parts_2, grads_1),
        "expert", scatter_dimension=0, axis_index_groups=SAME_CORE, tiled=False,
    )
    grad_in_one, mine_1, other_1 = whole(
        last_kernel,
        (shape(ROWS, WIDTH, kind=f32), shape(WIDTH, WIDE), shape(WIDTH, WIDE)),
        scratch=GRAD_SCRATCH,
        flops=8e9,
        raw=2,
        urgent=6,
    )(
        *weights_one, target_one, gate_1, middle_1, grad_one, answers_1,
        part(grad_buffer, 0, PLACES), rows_one,
        packed_1, attend_1, mixed_1,
    )

    got_grad = swap_sections(pick(grad_in_two, grad_in_one)[:SEQ].astype(bf16))
    grad_inputs = stack_micros(section.reshape(1), grad_in_one, grad_in_two, got_grad)

    def add_eight(got):
        return jnp.sum(got.astype(f32), axis=0).astype(bf16)

    parts = add_parts(mine_1, swap_cores(other_1), (WIDE,))[0]
    dp_one = dp.reshape(1).astype(jnp.int32)
    pieces = slice_grads(dp_one, expert_rows, expert_weights, (parts,))
    pieces = [pieces[0]] + [shift_dp(pieces[by], by) for by in (1, 2, 3)]
    grad_expert_in, grad_expert_out = expert_outputs(dp_one, pieces)
    parts = jnp.stack([add_eight(spread_parts(parts)), summed_2])
    got = lax.all_to_all(
        parts.reshape(8, 24, WIDE), ("section", "dp"), split_axis=0, concat_axis=0, tiled=True
    )
    total = jnp.sum(got.astype(f32), axis=0).astype(bf16)
    total = tie(total, got_grad)
    own = lax.all_to_all(
        jnp.broadcast_to(total[None], (8, 24, WIDE)),
        "expert", split_axis=0, concat_axis=0, tiled=True, axis_index_groups=SAME_CORE,
    ).reshape(192, WIDE)
    own = tie(own, section_outputs, grad_inputs, grad_expert_in)
    other = swap_cores(own)
    grad_qkv, grad_out, grad_router, grad_norms = halves_outputs(
        which, own, other, ()
    )
    return (
        section_outputs.transpose(1, 0, 2)[None],
        grad_inputs.transpose(1, 0, 2)[None],
        grad_qkv[None],
        grad_out[None],
        grad_router.T[None],
        grad_norms[None],
        grad_expert_in[None, None],
        grad_expert_out.T[None, None],
    )


def solution(mesh):
    tokens = P(None, ("dp", "expert"), None)
    tables = P("section", None, ("dp", "expert"), None)
    rows = P("section", "dp", None)
    norms = P("section", None, "dp")
    into = P("section", "expert", "dp", None)
    back = P("section", "expert", None, "dp")
    return jax.shard_map(
        shards,
        mesh=mesh,
        in_specs=(tokens, tokens, rows, rows, rows, norms, into, back, tables, tables, tables),
        out_specs=(tables, tables, rows, rows, rows, norms, into, back),
        check_vma=False,
    )
```

```python
import functools

import jax
import jax.numpy as jnp
from jax import lax
from jax.experimental import pallas as pl
from jax.experimental.pallas import tpu as pltpu
from jax.sharding import PartitionSpec as P

WIDTH = 768
HDIM = 64
SEQ = 197
ROWS = 208
EXPERTS = 16
SLOTS = 8
PLACES = EXPERTS * SLOTS
HIDDEN = 3072
EPSILON = 1e-06
SCALE = HDIM ** (-0.5)
HEADS = WIDTH // HDIM
PAIRS = HEADS // 2
HALF = 1536
EXTRA = 128
WIDE = HALF + EXTRA
BLOCK = 1024
STEPS = HIDDEN // BLOCK
VMEM = 56 * 1024 * 1024
SECTION_EXPERT = ("section", "expert")

bf16 = jnp.bfloat16
f32 = jnp.float32


def mm(a, b, contract=(1, 0)):
    return lax.dot_general(
        a, b, (((contract[0],), (contract[1],)), ((), ())), preferred_element_type=f32
    )


def normalize(rows):
    centred = rows - jnp.mean(rows, axis=-1, keepdims=True)
    factor = lax.rsqrt(jnp.mean(centred * centred, axis=-1, keepdims=True) + EPSILON)
    return centred * factor, factor


def norm_backward(grad, normal, factor, gain):
    scaled = grad * gain
    inner = (
        scaled
        - jnp.mean(scaled, axis=-1, keepdims=True)
        - normal * jnp.mean(scaled * normal, axis=-1, keepdims=True)
    )
    return factor * inner


def gelu_parts(pre):
    cdf = 0.5 * (1.0 + lax.erf(pre * 0.7071067811865476))
    return cdf


def gelu_slope(pre, cdf):
    return cdf + pre * (0.3989422804014327 * jnp.exp(-0.5 * pre * pre))


def extras_of(weights):
    return weights("extra").astype(f32).T


def selection(target_ref):
    places = lax.broadcasted_iota(jnp.int32, (PLACES, ROWS), 0)
    return (places == target_ref[0:1, :]) | (places == target_ref[1:2, :])


def slot_gates(chosen, gate_t):
    spread = jnp.broadcast_to(gate_t[:, None, :], (EXPERTS, SLOTS, ROWS)).reshape(PLACES, ROWS)
    return jnp.sum(jnp.where(chosen, spread, 0.0), axis=1, keepdims=True)


def low_lanes():
    return lax.broadcasted_iota(jnp.int32, (ROWS, 2 * HDIM), 1) < HDIM


def combine(middle, chosen, gate_t, answers):
    weighted = slot_gates(chosen, gate_t) * answers
    high = weighted.astype(bf16)
    low = (weighted - high.astype(f32)).astype(bf16)
    pick = chosen.astype(f32).astype(bf16)
    return middle + mm(pick, high, (0, 0)) + mm(pick, low, (0, 0))


def attention_forward(rows, weights, target, packed, mixed, middle_out, attend_out, gate):
    extras = extras_of(weights)
    normal, _ = normalize(rows)
    normed = (normal * extras[16:17] + extras[17:18]).astype(bf16)
    packed_ref, mixed_ref, attend_ref = packed.ref, mixed.ref, attend_out.ref
    for number, name in enumerate("qkv"):
        columns = slice(number * WIDTH, (number + 1) * WIDTH)
        packed_ref[:, columns] = mm(normed, weights(name)).astype(bf16)
    packed.send()
    lower = low_lanes()
    inside = lax.broadcasted_iota(jnp.int32, (ROWS, ROWS), 1) < SEQ
    for pair in range(PAIRS):
        at = pair * 128
        queries = packed_ref[:, at : at + 128]
        keys = packed_ref[:, WIDTH + at : WIDTH + at + 128]
        values = packed_ref[:, 2 * WIDTH + at : 2 * WIDTH + at + 128]
        outs = []
        for side in range(2):
            mine = lower if side == 0 else jnp.logical_not(lower)
            scores = mm(jnp.where(mine, queries, jnp.zeros_like(queries)), keys, (1, 1)) * SCALE
            scores = jnp.where(inside, scores, -1e30)
            highest = jnp.max(scores, axis=-1, keepdims=True)
            expo = jnp.exp(scores - highest)
            total = jnp.sum(expo, axis=-1, keepdims=True)
            attend = (expo * (1.0 / total)).astype(bf16)
            attend_ref[2 * pair + side] = attend
            outs.append(mm(attend, values))
        mixed_ref[:, at : at + 128] = jnp.where(lower, outs[0], outs[1]).astype(bf16)
    attend_out.send()
    mixed.send()
    middle = rows + mm(mixed_ref[...], weights("out"))
    middle_out.ref[...] = middle
    middle_out.send()
    normal, _ = normalize(middle)
    second = (normal * extras[18:19] + extras[19:20]).astype(bf16)
    logits = mm(extras[0:EXPERTS].astype(bf16), second, (1, 1))
    expo = jnp.exp(logits - jnp.max(logits, axis=0, keepdims=True))
    gate_t = expo / jnp.sum(expo, axis=0, keepdims=True)
    gate.ref[...] = gate_t
    gate.send()
    chosen = selection(target())
    buffer = mm(chosen.astype(f32).astype(bf16), second)
    return chosen, gate_t, buffer


def backward_heads(
    grad_out, answers, grad_buffer, target, gate, middle, packed, attend_in, mixed, weights, pair_out,
    branch_ref, packed_grad_ref, mixed_grad_ref,
):
    gate_t = gate()[...]
    chosen = selection(target())
    pick_wide = chosen.astype(f32)
    pick = pick_wide.astype(bf16)
    arrived = mm(pick, grad_out.astype(bf16))
    grad_gates = jnp.sum(arrived * answers, axis=1, keepdims=True)
    grad_probs = jnp.sum((pick_wide * grad_gates).reshape(EXPERTS, SLOTS, ROWS), axis=1)
    grad_logits = gate_t * (grad_probs - jnp.sum(grad_probs * gate_t, axis=0, keepdims=True))
    grad_logits = grad_logits.astype(bf16)
    normal, factor = normalize(middle()[...])
    extras = extras_of(weights)
    second = (normal * extras[18:19] + extras[19:20]).astype(bf16)
    grad_router = mm(grad_logits, second)
    grad_second = mm(grad_logits, extras[0:EXPERTS].astype(bf16), (0, 0)) + mm(
        pick, grad_buffer, (0, 0)
    )
    gain_two = jnp.sum(grad_second * normal, axis=0, keepdims=True)
    shift_two = jnp.sum(grad_second, axis=0, keepdims=True)
    grad_middle = grad_out + norm_backward(grad_second, normal, factor, extras[18:19])
    branch_ref[...] = grad_middle.astype(bf16)
    mixed_grad_ref[...] = mm(branch_ref[...], weights("out"), (1, 1)).astype(bf16)
    pair_out.put(1, WIDTH, mm(mixed()[...], branch_ref[...], (0, 0)))
    lower = low_lanes()
    packed_ref, attend_ref = packed(), attend_in()
    for pair in range(PAIRS):
        at = pair * 128
        queries = packed_ref[:, at : at + 128]
        keys = packed_ref[:, WIDTH + at : WIDTH + at + 128]
        values = packed_ref[:, 2 * WIDTH + at : 2 * WIDTH + at + 128]
        upstream = mixed_grad_ref[:, at : at + 128]
        sums = [0.0, 0.0, 0.0]
        for side in range(2):
            mine = lower if side == 0 else jnp.logical_not(lower)
            zero = jnp.zeros_like(queries)
            upstream_one = jnp.where(mine, upstream, zero)
            attend_low = attend_ref[2 * pair + side]
            attend = attend_low.astype(f32)
            grad_attend = mm(upstream_one, values, (1, 1))
            inner = jnp.sum(grad_attend * attend, axis=-1, keepdims=True)
            grad_scores = (attend * (grad_attend - inner)).astype(bf16)
            sums[0] += mm(grad_scores, jnp.where(mine, keys, zero))
            sums[1] += mm(grad_scores, jnp.where(mine, queries, zero), (0, 0))
            sums[2] += mm(attend_low, upstream_one, (0, 0))
        packed_grad_ref[:, at : at + 128] = (sums[0] * SCALE).astype(bf16)
        packed_grad_ref[:, WIDTH + at : WIDTH + at + 128] = (sums[1] * SCALE).astype(bf16)
        packed_grad_ref[:, 2 * WIDTH + at : 2 * WIDTH + at + 128] = sums[2].astype(bf16)
    return grad_middle, extras, (grad_router, gain_two, shift_two)


def backward_rows(grad_middle, extras, small, normal_pair, weights, packed_grad_ref):
    normal, factor = normal_pair
    grad_normed = 0.0
    for number, name in enumerate("qkv"):
        columns = slice(number * WIDTH, (number + 1) * WIDTH)
        grad_normed += mm(packed_grad_ref[:, columns], weights(name), (1, 1))
    gain_one = jnp.sum(grad_normed * normal, axis=0, keepdims=True)
    shift_one = jnp.sum(grad_normed, axis=0, keepdims=True)
    grad_router, gain_two, shift_two = small
    gathered = jnp.concatenate(
        [
            grad_router,
            gain_one,
            shift_one,
            gain_two,
            shift_two,
            jnp.zeros((EXTRA - EXPERTS - 4, WIDTH), f32),
        ],
        axis=0,
    )
    return grad_middle + norm_backward(grad_normed, normal, factor, extras[16:17]), gathered


class Pair:
    def __init__(self, which, ref, mine_ref, send_ref, sems):
        self.which, self.ref, self.sems = which, ref, sems
        self.mine_ref, self.send_ref = mine_ref, send_ref
        self.copies = []

    def put(self, half, start, value):
        columns = slice(start, start + value.shape[1])
        self.ref[half, :, columns] = value.astype(bf16)
        near, sem = self.ref.at[half, :, columns], self.sems.at[len(self.copies)]
        mine = pltpu.make_async_copy(near, self.mine_ref.at[:, columns], sem)
        send = pltpu.make_async_copy(near, self.send_ref.at[:, columns], sem)
        pl.when(self.which == half)(mine.start)
        pl.when(self.which != half)(send.start)
        self.copies.append(mine)

    def main(self, normed, packed_grad_ref):
        self.put(0, 0, mm(normed, packed_grad_ref[:, 0:WIDTH], (0, 0)))
        self.put(0, WIDTH, mm(normed, packed_grad_ref[:, WIDTH:HALF], (0, 0)))
        self.put(1, 0, mm(normed, packed_grad_ref[:, HALF:], (0, 0)))

    def rest(self, gathered):
        self.put(0, HALF, gathered.T)
        self.put(1, HALF, jnp.zeros((WIDTH, EXTRA), f32))

    def wait(self):
        for copy in self.copies:
            copy.wait()


def normed_rows(rows, extras):
    normal, factor = normalize(rows)
    return (normal, factor), (normal * extras[16:17] + extras[17:18]).astype(bf16)


class Arriving:
    def __init__(self, far, near, sem):
        self.copy, self.near, self.pending = pltpu.make_async_copy(far, near, sem), near, True
        self.copy.start()

    def __call__(self):
        if self.pending:
            self.copy.wait()
            self.pending = False
        return self.near


class Leaving:
    def __init__(self, far, near, sem):
        self.copy, self.ref, self.sent = pltpu.make_async_copy(near, far, sem), near, False

    def send(self):
        if not self.sent:
            self.copy.start()
            self.sent = True


CHUNKS = {
    "q": (0, 0, WIDTH),
    "k": (0, WIDTH, WIDTH),
    "extra": (0, HALF, EXTRA),
    "v": (1, 0, WIDTH),
    "out": (1, WIDTH, WIDTH),
}


class Weights:
    def __init__(self, which, own_ref, other_ref, near_ref, sems):
        self.near, self.pending, self.copies = near_ref, [0, 1], []
        for half in range(2):
            copies = [
                pltpu.make_async_copy(source, near_ref.at[half], sems.at[half])
                for source in (own_ref, other_ref)
            ]
            pl.when(which == half)(copies[0].start)
            pl.when(which != half)(copies[1].start)
            self.copies.append(copies[0])

    def __call__(self, name):
        half, start, width = CHUNKS[name]
        if half in self.pending:
            self.copies[half].wait()
            self.pending.remove(half)
        return self.near[half, :, start : start + width]


def first_kernel(which, weights, ins, outs, scratch):
    rows, target = ins
    send = outs[5]
    _, _, buffer = attention_forward(rows()[...].astype(f32), weights, target, *outs[:5])
    send.ref[0:PLACES] = buffer.astype(bf16)
    send.ref[PLACES:] = jnp.zeros((PLACES, WIDTH), bf16)


def second_kernel(which, weights, ins, outs, scratch):
    middle_in, gate_in, target_in, answers, grad, target = ins
    out_rows, send = outs[0], outs[6]
    out = combine(
        middle_in()[...], selection(target_in()), gate_in()[...], answers()[...].astype(f32)
    )
    out_rows.ref[...] = out.astype(bf16)
    out_rows.send()
    chosen, gate_t, buffer = attention_forward(
        out.astype(bf16).astype(f32), weights, target, *outs[1:6]
    )
    arrived = mm(chosen.astype(f32).astype(bf16), grad()[...])
    grad_answers = slot_gates(chosen, gate_t) * arrived
    both = jnp.concatenate(
        [
            buffer.reshape(EXPERTS, SLOTS, WIDTH),
            grad_answers.reshape(EXPERTS, SLOTS, WIDTH),
        ],
        axis=1,
    ).reshape(2 * PLACES, WIDTH)
    send.ref[0 : 2 * PLACES] = jnp.zeros((2 * PLACES, WIDTH), bf16)
    send.ref[2 * PLACES :] = both.astype(bf16)


def third_kernel(which, weights, ins, outs, scratch):
    back, target, gate, middle, grad, rows, packed, attend, mixed, target_next, gate_next = ins
    out_rows, grad_in_out, grad_low_out, send, mine_ref, other_grad_ref = outs
    mixed_grad_ref, packed_grad_ref, branch_ref, pair_ref, pair_sems = scratch
    pair = Pair(which, pair_ref, mine_ref, other_grad_ref, pair_sems)
    both = back()[...].astype(f32).reshape(EXPERTS, 2 * SLOTS, WIDTH)
    answers = both[:, :SLOTS].reshape(PLACES, WIDTH)
    grad_buffer = both[:, SLOTS:].reshape(PLACES, WIDTH).astype(bf16)
    out = combine(middle()[...], selection(target()), gate()[...], answers)
    out_rows.ref[...] = out.astype(bf16)
    out_rows.send()
    grad_middle, extras, small = backward_heads(
        grad()[...].astype(f32), answers, grad_buffer, target, gate, middle, packed, attend,
        mixed, weights, pair, branch_ref, packed_grad_ref, mixed_grad_ref,
    )
    normal_pair, normed = normed_rows(rows()[...].astype(f32), extras)
    pair.main(normed, packed_grad_ref)
    grad_in, gathered = backward_rows(
        grad_middle, extras, small, normal_pair, weights, packed_grad_ref
    )
    pair.rest(gathered)
    grad_in_out.ref[...] = grad_in
    grad_in_out.send()
    grad_low = grad_in.astype(bf16)
    grad_low_out.ref[...] = grad_low
    grad_low_out.send()
    chosen = selection(target_next())
    arrived = mm(chosen.astype(f32).astype(bf16), grad_low)
    send.ref[0:PLACES] = (slot_gates(chosen, gate_next()[...]) * arrived).astype(bf16)
    send.ref[PLACES:] = jnp.zeros((PLACES, WIDTH), bf16)
    send.send()
    pair.wait()


def last_kernel(which, weights, ins, outs, scratch):
    target, gate, middle, grad, answers, grad_buffer, rows, packed, attend, mixed = ins
    grad_in_out, mine_ref, other_grad_ref = outs
    mixed_grad_ref, packed_grad_ref, branch_ref, pair_ref, pair_sems = scratch
    pair = Pair(which, pair_ref, mine_ref, other_grad_ref, pair_sems)
    grad_middle, extras, small = backward_heads(
        grad()[...].astype(f32), answers()[...].astype(f32), grad_buffer()[...], target, gate,
        middle, packed, attend, mixed, weights, pair, branch_ref, packed_grad_ref, mixed_grad_ref,
    )
    normal_pair, normed = normed_rows(rows()[...].astype(f32), extras)
    pair.main(normed, packed_grad_ref)
    grad_in_out.ref[...], gathered = backward_rows(
        grad_middle, extras, small, normal_pair, weights, packed_grad_ref
    )
    grad_in_out.send()
    pair.rest(gathered)
    pair.wait()


def shape(*sizes, kind=bf16):
    return jax.ShapeDtypeStruct(sizes, kind)


SAVED = (
    shape(ROWS, 3 * WIDTH),
    shape(ROWS, WIDTH),
    shape(ROWS, WIDTH, kind=f32),
    shape(HEADS, ROWS, ROWS),
    shape(EXPERTS, ROWS, kind=f32),
)
WEIGHT_SCRATCH = [
    pltpu.VMEM((2, WIDTH, WIDE), bf16),
    pltpu.SemaphoreType.DMA((2,)),
]
GRAD_SCRATCH = [
    pltpu.VMEM((ROWS, WIDTH), bf16),
    pltpu.VMEM((ROWS, 3 * WIDTH), bf16),
    pltpu.VMEM((ROWS, WIDTH), bf16),
    pltpu.VMEM((2, WIDTH, WIDE), bf16),
    pltpu.SemaphoreType.DMA((6,)),
]


def ignoring(kernel, at, count):
    def run(*refs):
        kernel(*refs[:at], *refs[at + count :])

    return run


ANYWHERE = pl.BlockSpec(memory_space=pl.ANY)


IN_HBM = pl.BlockSpec(memory_space=pltpu.HBM)


def part(array, start, rows):
    return array, start, rows


def operands(args):
    parts = [each if isinstance(each, tuple) else (each, 0, each.shape[0]) for each in args]
    arrays = [array for array, _, _ in parts]
    slices = [pl.ds(start, rows) for _, start, rows in parts]
    scratch = [
        pltpu.VMEM((rows,) + array.shape[1:], array.dtype) for array, _, rows in parts
    ]
    return arrays, slices, scratch


def whole(kernel, outs, scratch=(), flops=4e9, raw=0, urgent=2, earlier=()):
    def call(which, own, other, *args):
        count, made = len(args), len(outs) - raw
        arrays, slices, buffers = operands(args)

        def run(*refs):
            which_ref, own_ref, other_ref, *refs = refs
            far, refs = refs[:count], refs[count + len(earlier) :]
            results, refs = refs[: len(outs)], refs[len(outs) :]
            weights_ref, sems, in_sems, out_sems, *refs = refs
            near, refs = refs[:count], refs[count:]
            kept, rest = refs[:made], refs[made:]

            def arrive(places):
                return [Arriving(far[i].at[slices[i]], near[i], in_sems.at[i]) for i in places]

            arriving = arrive(range(urgent))
            weights = Weights(which_ref[0], own_ref, other_ref, weights_ref, sems)
            arriving += arrive(range(urgent, count))
            leaving = [Leaving(results[i], kept[i], out_sems.at[i]) for i in range(made)]
            kernel(which_ref[0], weights, arriving, leaving + list(results[made:]), rest)
            for each in leaving:
                each.send()
            for each in leaving:
                each.copy.wait()

        return pl.pallas_call(
            run,
            out_shape=outs,
            in_specs=[pl.BlockSpec(memory_space=pltpu.SMEM)]
            + [IN_HBM] * (2 + count)
            + [ANYWHERE] * len(earlier),
            out_specs=(IN_HBM,) * len(outs),
            scratch_shapes=WEIGHT_SCRATCH
            + [pltpu.SemaphoreType.DMA((count,)), pltpu.SemaphoreType.DMA((max(made, 1),))]
            + buffers
            + [pltpu.VMEM(each.shape, each.dtype) for each in outs[:made]]
            + list(scratch),
            compiler_params=pltpu.CompilerParams(vmem_limit_bytes=VMEM),
            cost_estimate=pl.CostEstimate(
                flops=int(flops), bytes_accessed=12_000_000, transcendentals=600_000
            ),
        )(which, own, other, *arrays, *earlier)

    return call


ITEMS = 2 * EXPERTS * SLOTS


def answer_kernel(blocks, ins, outs, scratch):
    (items,), (out,), (total,) = ins, outs, scratch
    rows = items()[...]
    for step in range(STEPS):
        w_in, w_back = blocks(step)
        pre = mm(rows, w_in)
        hidden = (pre * gelu_parts(pre)).astype(bf16)
        part = mm(hidden, w_back, (1, 1))
        total[...] = part if step == 0 else total[...] + part
    out.ref[...] = total[...].astype(bf16)


def both_kernel(blocks, ins, outs, scratch):
    (mixed,), (out,), (items, grads, total, total_grad) = ins, outs, scratch
    rows = mixed()[...].astype(f32).reshape(ITEMS // SLOTS, 2 * SLOTS, WIDTH)
    items[...] = rows[:, :SLOTS].reshape(ITEMS, WIDTH).astype(bf16)
    grads[...] = rows[:, SLOTS:].reshape(ITEMS, WIDTH).astype(bf16)
    for step in range(STEPS):
        w_in, w_back = blocks(step)
        pre = mm(items[...], w_in)
        cdf = gelu_parts(pre)
        grad_hidden = mm(grads[...], w_back)
        part = mm((pre * cdf).astype(bf16), w_back, (1, 1))
        grad_pre = (grad_hidden * gelu_slope(pre, cdf)).astype(bf16)
        part_grad = mm(grad_pre, w_in, (1, 1))
        total[...] = part if step == 0 else total[...] + part
        total_grad[...] = part_grad if step == 0 else total_grad[...] + part_grad
    both = jnp.concatenate(
        [
            total[...].reshape(ITEMS // SLOTS, SLOTS, WIDTH),
            total_grad[...].reshape(ITEMS // SLOTS, SLOTS, WIDTH),
        ],
        axis=1,
    )
    out.ref[...] = both.reshape(2 * ITEMS, WIDTH).astype(bf16)


def grads_kernel(blocks, ins, outs, scratch):
    (items, grads), (out,), (total,) = ins, outs, scratch
    rows, grad_rows = items()[...], grads()[...]
    for step in range(STEPS):
        w_in, w_back = blocks(step)
        pre = mm(rows, w_in)
        grad_hidden = mm(grad_rows, w_back)
        grad_pre = (grad_hidden * gelu_slope(pre, gelu_parts(pre))).astype(bf16)
        part = mm(grad_pre, w_in, (1, 1))
        total[...] = part if step == 0 else total[...] + part
    out.ref[...] = total[...].astype(bf16)


SLICE = HIDDEN // 4
GROUP = 256


def slice_kernel(
    dp_ref, rows_ref, w_ref, *refs
):
    outs, refs = refs[:4], refs[4:]
    rows_near, w_near, items, grads, turned, made, sems, out_sems = refs
    at = dp_ref[0]
    arriving = [
        Arriving(
            w_ref.at[:, pl.ds(pl.multiple_of(side * HIDDEN + at * SLICE, 128), SLICE)],
            w_near.at[side],
            sems.at[side],
        )
        for side in range(2)
    ]
    blocks = [
        Arriving(rows_ref.at[pl.ds(i * 2 * ITEMS, 2 * ITEMS)], rows_near.at[i], sems.at[2 + i])
        for i in range(4)
    ]
    for i in range(4):
        rows = blocks[i]()[...].astype(f32).reshape(ITEMS // SLOTS, 2 * SLOTS, WIDTH)
        place = slice(i * ITEMS, (i + 1) * ITEMS)
        for side, into in enumerate((items, grads)):
            mine = rows[:, side * SLOTS : (side + 1) * SLOTS].reshape(ITEMS, WIDTH).astype(bf16)
            into[place] = mine
            turned[side, :, place] = mine.T
    w_in, w_back = arriving[0](), arriving[1]()
    for start in range(0, SLICE, GROUP):
        columns = slice(start, start + GROUP)
        pre = mm(items[...], w_in[:, columns])
        cdf = gelu_parts(pre)
        grad_hidden = mm(grads[...], w_back[:, columns])
        grad_pre = (grad_hidden * gelu_slope(pre, cdf)).astype(bf16)
        hidden = (pre * cdf).astype(bf16)
        made[:, columns] = mm(turned[0], grad_pre).astype(bf16)
        made[:, SLICE + start : SLICE + start + GROUP] = mm(turned[1], hidden).astype(bf16)
    copies = []
    for by in range(4):
        rows = pl.ds(pl.multiple_of(lax.rem(at + by, 4) * 192, 16), 192)
        copies.append(pltpu.make_async_copy(made.at[rows], outs[by], out_sems.at[by]))
        copies[-1].start()
    for copy in copies:
        copy.wait()


def slice_grads(dp, rows, weights, earlier):
    return pl.pallas_call(
        ignoring(slice_kernel, 3, len(earlier)),
        out_shape=(shape(192, 2 * SLICE),) * 4,
        in_specs=[pl.BlockSpec(memory_space=pltpu.SMEM)]
        + [IN_HBM] * 2
        + [ANYWHERE] * len(earlier),
        out_specs=(IN_HBM,) * 4,
        scratch_shapes=[
            pltpu.VMEM((4, 2 * ITEMS, WIDTH), bf16),
            pltpu.VMEM((2, WIDTH, SLICE), bf16),
            pltpu.VMEM((4 * ITEMS, WIDTH), bf16),
            pltpu.VMEM((4 * ITEMS, WIDTH), bf16),
            pltpu.VMEM((2, WIDTH, 4 * ITEMS), bf16),
            pltpu.VMEM((WIDTH, 2 * SLICE), bf16),
            pltpu.SemaphoreType.DMA((6,)),
            pltpu.SemaphoreType.DMA((4,)),
        ],
        compiler_params=pltpu.CompilerParams(vmem_limit_bytes=VMEM),
        cost_estimate=pl.CostEstimate(
            flops=5_000_000_000, bytes_accessed=9_000_000, transcendentals=800_000
        ),
    )(dp, rows, weights, *earlier)


def spread_kernel(dp_ref, *refs):
    pieces, (in_ref, out_ref) = refs[:4], refs[4:]
    for by, ref in enumerate(pieces):
        at = lax.rem(dp_ref[0] - by + 4, 4)
        columns = pl.ds(pl.multiple_of(at * SLICE, 128), SLICE)
        in_ref[:, columns] = ref[:, :SLICE].astype(f32)
        out_ref[:, columns] = ref[:, SLICE:].astype(f32)


def expert_outputs(dp, pieces):
    return pl.pallas_call(
        spread_kernel,
        out_shape=(shape(192, HIDDEN, kind=f32), shape(192, HIDDEN, kind=f32)),
        in_specs=[pl.BlockSpec(memory_space=pltpu.SMEM)]
        + [pl.BlockSpec(memory_space=pltpu.VMEM)] * 4,
        out_specs=(pl.BlockSpec(memory_space=pltpu.VMEM),) * 2,
        compiler_params=pltpu.CompilerParams(vmem_limit_bytes=VMEM),
        cost_estimate=pl.CostEstimate(flops=0, bytes_accessed=7_000_000, transcendentals=0),
    )(dp, *pieces)


def add_parts(mine, got, widths):
    def run(mine_ref, got_ref, *refs):
        results, refs = refs[: len(widths)], refs[len(widths) :]
        mine_near, got_near, in_sems, out_sems, *made = refs
        arriving = [
            [
                Arriving(far.at[:, j], near.at[j], in_sems.at[2 * j + side])
                for side, (far, near) in enumerate(((mine_ref, mine_near), (got_ref, got_near)))
            ]
            for j in range(8)
        ]
        copies = []
        for j in range(8):
            one, two = [each()[...].astype(f32) for each in arriving[j]]
            total = (one + two).astype(bf16)
            start = 0
            for number, width in enumerate(widths):
                made[number][j] = total[:, :, start : start + width]
                copies.append(
                    pltpu.make_async_copy(
                        made[number].at[j], results[number].at[j], out_sems.at[len(copies)]
                    )
                )
                copies[-1].start()
                start += width
        for copy in copies:
            copy.wait()

    return pl.pallas_call(
        run,
        out_shape=tuple(shape(8, 4, 24, width) for width in widths),
        in_specs=[ANYWHERE] * 2,
        out_specs=(IN_HBM,) * len(widths),
        scratch_shapes=[
            pltpu.VMEM((8, 4, 24, WIDE), bf16),
            pltpu.VMEM((8, 4, 24, WIDE), bf16),
            pltpu.SemaphoreType.DMA((16,)),
            pltpu.SemaphoreType.DMA((8 * len(widths),)),
        ]
        + [pltpu.VMEM((8, 4, 24, width), bf16) for width in widths],
        compiler_params=pltpu.CompilerParams(vmem_limit_bytes=VMEM),
        cost_estimate=pl.CostEstimate(flops=0, bytes_accessed=8_000_000, transcendentals=0),
    )(mine.reshape(4, 8, 24, WIDE), got.reshape(4, 8, 24, WIDE))


def tie(array, *earlier):
    return pl.pallas_call(
        lambda *refs: None,
        out_shape=jax.ShapeDtypeStruct(array.shape, array.dtype),
        in_specs=[IN_HBM] + [ANYWHERE] * len(earlier),
        out_specs=IN_HBM,
        input_output_aliases={0: 0},
        cost_estimate=pl.CostEstimate(flops=0, bytes_accessed=0, transcendentals=0),
    )(array, *earlier)


def place_kernel(at_ref, *refs):
    pieces, out_ref = refs[:4], refs[4]
    for number, by in enumerate((0, 1, 3, 2)):
        at = lax.rem(at_ref[0] - by + 4, 4)
        out_ref[:, pl.ds(at, 1)] = pieces[number][...][:, None]


def place(at, pieces, earlier):
    first, *sizes = pieces[0].shape
    return pl.pallas_call(
        ignoring(place_kernel, 5, len(earlier)),
        out_shape=shape(first, 4, *sizes),
        in_specs=[pl.BlockSpec(memory_space=pltpu.SMEM)]
        + [pl.BlockSpec(memory_space=pltpu.VMEM)] * 4
        + [ANYWHERE] * len(earlier),
        out_specs=pl.BlockSpec(memory_space=pltpu.VMEM),
        cost_estimate=pl.CostEstimate(flops=0, bytes_accessed=6_000_000, transcendentals=0),
    )(at, *pieces, *earlier)


def halves_kernel(which_ref, own_ref, other_ref, qkv_ref, out_ref, router_ref, norms_ref):
    def write(a_ref, b_ref):
        qkv_ref[:, :HALF] = a_ref[:, :HALF].astype(f32)
        qkv_ref[:, HALF:] = b_ref[:, :WIDTH].astype(f32)
        out_ref[...] = b_ref[:, WIDTH:HALF].astype(f32)
        extra = a_ref[:, HALF:].astype(f32).T
        router_ref[...] = extra[:EXPERTS]
        norms_ref[...] = extra[EXPERTS : EXPERTS + 4]

    @pl.when(which_ref[0] == 0)
    def _():
        write(own_ref, other_ref)

    @pl.when(which_ref[0] != 0)
    def _():
        write(other_ref, own_ref)


def halves_outputs(which, own, other, earlier):
    rows = own.shape[0]
    memories = (pltpu.SMEM, pltpu.VMEM, pltpu.VMEM)
    return pl.pallas_call(
        ignoring(halves_kernel, 3, len(earlier)),
        out_shape=(
            shape(rows, 3 * WIDTH, kind=f32),
            shape(rows, WIDTH, kind=f32),
            shape(EXPERTS, rows, kind=f32),
            shape(4, rows, kind=f32),
        ),
        in_specs=[pl.BlockSpec(memory_space=space) for space in memories]
        + [ANYWHERE] * len(earlier),
        out_specs=tuple(pl.BlockSpec(memory_space=pltpu.VMEM) for _ in range(4)),
    )(which, own, other, *earlier)


def copies_kernel(got_ref, out_ref):
    total = got_ref[0].astype(f32)
    for j in range(1, 8):
        total += got_ref[j].astype(f32)
    for j in range(8):
        out_ref[j] = total.astype(bf16)


def add_and_copy(got, earlier):
    return pl.pallas_call(
        ignoring(copies_kernel, 1, len(earlier)),
        out_shape=shape(8, 24, WIDE),
        in_specs=[pl.BlockSpec(memory_space=pltpu.VMEM)] + [ANYWHERE] * len(earlier),
        out_specs=pl.BlockSpec(memory_space=pltpu.VMEM),
        cost_estimate=pl.CostEstimate(flops=0, bytes_accessed=1_300_000, transcendentals=0),
    )(got, *earlier)


def stack_kernel(flag_ref, zero_ref, one_ref, got_ref, out_ref):
    @pl.when(flag_ref[0] == 0)
    def _():
        out_ref[:, 0, :] = zero_ref[0:SEQ, :]
        out_ref[:, 1, :] = got_ref[...].astype(f32)

    @pl.when(flag_ref[0] != 0)
    def _():
        out_ref[:, 0, :] = got_ref[...].astype(f32)
        out_ref[:, 1, :] = one_ref[0:SEQ, :]


def stack_micros(flag, zero, one, got):
    memories = (pltpu.SMEM, pltpu.VMEM, pltpu.VMEM, pltpu.VMEM)
    return pl.pallas_call(
        stack_kernel,
        out_shape=shape(SEQ, 2, WIDTH, kind=f32),
        in_specs=[pl.BlockSpec(memory_space=space) for space in memories],
        out_specs=pl.BlockSpec(memory_space=pltpu.VMEM),
        cost_estimate=pl.CostEstimate(flops=0, bytes_accessed=3_000_000, transcendentals=0),
    )(flag, zero, one, got)


def expert_call(kernel, args, weights, outs, scratch, flops, raw=0, earlier=(), flags=()):
    count, made = len(args), len(outs) - raw

    def run(*refs):
        scalars, refs = [ref[0] for ref in refs[: len(flags)]], refs[len(flags) :]
        far, refs = refs[:count], refs[count:]
        far_weights, refs = refs[0], refs[1 + len(earlier) :]
        results, refs = refs[: len(outs)], refs[len(outs) :]
        near_weights, sems, in_sems, out_sems, *refs = refs
        near, refs = refs[:count], refs[count:]
        kept, rest = refs[:made], refs[made:]
        arriving = [Arriving(far[i], near[i], in_sems.at[i]) for i in range(count)]
        parts = []
        for number in range(2 * STEPS):
            columns = pl.ds((number % 2) * HIDDEN + number // 2 * BLOCK, BLOCK)
            parts.append(
                Arriving(
                    far_weights.at[:, columns], near_weights.at[:, columns], sems.at[number]
                )
            )
        leaving = [Leaving(results[i], kept[i], out_sems.at[i]) for i in range(made)]

        def blocks(step):
            return parts[2 * step]()[...], parts[2 * step + 1]()[...]

        kernel(blocks, scalars + arriving, leaving + list(results[made:]), rest)
        for each in leaving:
            each.send()
        for each in leaving:
            each.copy.wait()

    return pl.pallas_call(
        run,
        out_shape=outs,
        in_specs=[pl.BlockSpec(memory_space=pltpu.SMEM)] * len(flags)
        + [IN_HBM] * (count + 1)
        + [ANYWHERE] * len(earlier),
        out_specs=(IN_HBM,) * len(outs),
        scratch_shapes=[
            pltpu.VMEM((WIDTH, 2 * HIDDEN), bf16),
            pltpu.SemaphoreType.DMA((2 * STEPS,)),
            pltpu.SemaphoreType.DMA((count,)),
            pltpu.SemaphoreType.DMA((made,)),
        ]
        + [pltpu.VMEM(each.shape, each.dtype) for each in args]
        + [pltpu.VMEM(each.shape, each.dtype) for each in outs[:made]]
        + list(scratch),
        compiler_params=pltpu.CompilerParams(vmem_limit_bytes=VMEM),
        cost_estimate=pl.CostEstimate(
            flops=int(flops), bytes_accessed=12_000_000, transcendentals=800_000
        ),
    )(*flags, *args, weights, *earlier)


TOTAL = pltpu.VMEM((ITEMS, WIDTH), f32)


def expert_answers(items, weights):
    return expert_call(
        answer_kernel, (items,), weights, (shape(ITEMS, WIDTH),), [TOTAL], 2.4e9
    )[0]


def expert_both(mixed, weights):
    rows = pltpu.VMEM((ITEMS, WIDTH), bf16)
    return expert_call(
        both_kernel, (mixed,), weights, (shape(2 * ITEMS, WIDTH),), [rows, rows, TOTAL, TOTAL], 4.8e9
    )[0]


def expert_grads(items, grads, weights):
    return expert_call(
        grads_kernel, (items, grads), weights, (shape(ITEMS, WIDTH),), [TOTAL], 3.6e9
    )[0]


def swap_sections(array):
    return lax.ppermute(array, "section", [(0, 1), (1, 0)])


def swap_cores(array):
    return lax.ppermute(array, "expert", [(i, i ^ 1) for i in range(EXPERTS)])


def shuffle(rows):
    return lax.all_to_all(rows, SECTION_EXPERT, split_axis=0, concat_axis=0, tiled=True)


def gather_dp(piece, me):
    out = jnp.zeros((4,) + piece.shape, piece.dtype)
    out = lax.dynamic_update_slice(out, piece[None], (me, 0, 0))
    for by in (1, 3, 2):
        out = lax.dynamic_update_slice(out, shift_dp(piece, by)[None], ((me - by) % 4, 0, 0))
    return out


def shift_dp(array, by):
    return lax.ppermute(array, "dp", [(i, (i + by) % 4) for i in range(4)])


def shift_z(array, by):
    pairs = [(i, i // 8 * 8 + (i % 8 + 2 * by) % 8) for i in range(EXPERTS)]
    return lax.ppermute(array, "expert", pairs)


SAME_CORE = [[core + 2 * i for i in range(8)] for core in (0, 1)]


def spread_parts(parts):
    return lax.all_to_all(
        parts, "expert", split_axis=0, concat_axis=0, tiled=True, axis_index_groups=SAME_CORE
    )


def shards(
    inputs, cotangent, qkv_weight, attn_out_weight, router_weight, norm_params, expert_in,
    expert_out, routes, slots, kept,
):
    section = lax.axis_index("section")
    first = section == 0
    core = lax.rem(lax.axis_index("expert"), 2)
    even = core == 0
    which = core.reshape(1).astype(jnp.int32)

    def pick(zero, one):
        return jnp.where(first, zero, one)

    expert_shard = jnp.concatenate([expert_in[0, 0], expert_out[0, 0].T], axis=1)
    expert_weights = lax.all_gather(expert_shard, "dp", axis=0, tiled=True)

    extra = jnp.concatenate(
        [
            router_weight[0],
            norm_params[0].T,
            jnp.zeros((router_weight.shape[1], EXTRA - EXPERTS - 4), bf16),
        ],
        axis=1,
    )
    mine = jnp.concatenate(
        [
            jnp.where(
                even,
                qkv_weight[0][:, :HALF],
                jnp.concatenate([qkv_weight[0][:, HALF:], attn_out_weight[0]], axis=1),
            ),
            extra,
        ],
        axis=1,
    )
    dp = lax.axis_index("dp")
    z = lax.rem(lax.axis_index("expert"), 8) // 2
    mine = lax.dynamic_slice(mine, (z * 48, 0), (48, WIDE))
    theirs = swap_sections(mine)

    over_dp_one = gather_dp(pick(mine, theirs), dp)
    over_dp_two = gather_dp(pick(theirs, mine), dp)

    def gather_z(piece):
        return [piece] + [shift_z(piece, by) for by in (1, 3, 2)]

    def halves(pieces, earlier):
        at = z.reshape(1).astype(jnp.int32)
        own = place(at, pieces, earlier).reshape(WIDTH, WIDE)
        return which, own, swap_cores(own)

    weights_one = halves(gather_z(over_dp_one), (over_dp_two,))

    target = jnp.where(kept[0] > 0, routes[0] * SLOTS + slots[0], -1)
    target = jnp.pad(
        target.transpose(0, 2, 1), ((0, 0), (0, 0), (0, ROWS - SEQ)), constant_values=-1
    )
    received = swap_sections(pick(target[1], target[0]))
    own = pick(target[0], target[1])
    target_one, target_two = pick(own, received), pick(received, own)

    edge = ((0, ROWS - SEQ), (0, 0))
    rows_one = jnp.pad(pick(inputs[0], inputs[1]), edge)
    grad_two = jnp.pad(pick(cotangent[0], cotangent[1]), edge)

    packed_1, mixed_1, middle_1, attend_1, gate_1, send = whole(
        first_kernel, SAVED + (shape(2 * PLACES, WIDTH),), urgent=1
    )(*weights_one, rows_one, target_one)
    items_1 = shuffle(send.reshape(32, SLOTS, WIDTH)).reshape(ITEMS, WIDTH)
    answers = expert_answers(items_1, expert_weights)
    weights_two = halves(gather_z(over_dp_two), (items_1,))
    answers_1 = shuffle(answers.reshape(32, SLOTS, WIDTH)).reshape(ITEMS, WIDTH)
    answers_1 = part(answers_1, 0, PLACES)

    rows_two, packed_2, mixed_2, middle_2, attend_2, gate_2, send = whole(
        second_kernel,
        (shape(ROWS, WIDTH),) + SAVED + (shape(4 * PLACES, WIDTH),),
        urgent=4,
    )(*weights_two, middle_1, gate_1, target_one, answers_1, grad_two, target_two)
    items_2 = shuffle(send.reshape(32, 2 * SLOTS, WIDTH)).reshape(2 * ITEMS, WIDTH)
    back = expert_both(items_2, expert_weights)
    back = shuffle(back.reshape(32, 2 * SLOTS, WIDTH)).reshape(2 * ITEMS, WIDTH)
    back = part(back, 2 * PLACES, 2 * PLACES)
    out_two, grad_in_two, grad_one, send, mine_2, other_2 = whole(
        third_kernel,
        (
            shape(ROWS, WIDTH),
            shape(ROWS, WIDTH, kind=f32),
            shape(ROWS, WIDTH),
            shape(2 * PLACES, WIDTH),
            shape(WIDTH, WIDE),
            shape(WIDTH, WIDE),
        ),
        scratch=GRAD_SCRATCH,
        flops=8e9,
        raw=2,
        urgent=5,
    )(
        *weights_two, back, target_two, gate_2, middle_2, grad_two, rows_two, packed_2, attend_2,
        mixed_2, target_one, gate_1,
    )

    got_out = swap_sections(pick(out_two, rows_two)[:SEQ])
    own_out = pick(rows_two, out_two)[:SEQ]
    section_outputs = jnp.stack([pick(own_out, got_out), pick(got_out, own_out)])

    grads_1 = shuffle(send.reshape(32, SLOTS, WIDTH)).reshape(ITEMS, WIDTH)
    parts_2 = add_parts(mine_2, swap_cores(other_2), (WIDE,))[0]
    back = expert_grads(items_1, grads_1, expert_weights)
    grad_buffer = shuffle(back.reshape(32, SLOTS, WIDTH)).reshape(ITEMS, WIDTH)
    mixed_one = jnp.concatenate(
        [items_1.reshape(32, SLOTS, WIDTH), grads_1.reshape(32, SLOTS, WIDTH)], axis=1
    )
    expert_rows = lax.all_gather(
        pick(mixed_one.reshape(2 * ITEMS, WIDTH), items_2), "dp", axis=0, tiled=True
    )
    summed_2 = lax.psum_scatter(
        tie(parts_2, grads_1),
        "expert", scatter_dimension=0, axis_index_groups=SAME_CORE, tiled=False,
    )
    grad_in_one, mine_1, other_1 = whole(
        last_kernel,
        (shape(ROWS, WIDTH, kind=f32), shape(WIDTH, WIDE), shape(WIDTH, WIDE)),
        scratch=GRAD_SCRATCH,
        flops=8e9,
        raw=2,
        urgent=6,
    )(
        *weights_one, target_one, gate_1, middle_1, grad_one, answers_1,
        part(grad_buffer, 0, PLACES), rows_one,
        packed_1, attend_1, mixed_1,
    )

    got_grad = swap_sections(pick(grad_in_two, grad_in_one)[:SEQ].astype(bf16))
    grad_inputs = stack_micros(section.reshape(1), grad_in_one, grad_in_two, got_grad)

    def add_eight(got):
        return jnp.sum(got.astype(f32), axis=0).astype(bf16)

    parts = add_parts(mine_1, swap_cores(other_1), (WIDE,))[0]
    dp_one = dp.reshape(1).astype(jnp.int32)
    pieces = slice_grads(dp_one, expert_rows, expert_weights, (parts,))
    pieces = [pieces[0]] + [shift_dp(pieces[by], by) for by in (1, 2, 3)]
    grad_expert_in, grad_expert_out = expert_outputs(dp_one, pieces)
    parts = jnp.stack([add_eight(spread_parts(parts)), summed_2])
    got = lax.all_to_all(
        parts.reshape(8, 24, WIDE), ("section", "dp"), split_axis=0, concat_axis=0, tiled=True
    )
    own = lax.all_to_all(
        add_and_copy(got, (pieces[0],)),
        "expert", split_axis=0, concat_axis=0, tiled=True, axis_index_groups=SAME_CORE,
    ).reshape(192, WIDE)
    own = tie(own, section_outputs, grad_inputs, grad_expert_in)
    other = swap_cores(own)
    grad_qkv, grad_out, grad_router, grad_norms = halves_outputs(
        which, own, other, ()
    )
    return (
        section_outputs[None],
        grad_inputs.transpose(1, 0, 2)[None],
        grad_qkv[None],
        grad_out[None],
        grad_router.T[None],
        grad_norms[None],
        grad_expert_in[None, None],
        grad_expert_out.T[None, None],
    )


def solution(mesh):
    tokens = P(None, ("dp", "expert"), None)
    tables = P("section", None, ("dp", "expert"), None)
    rows = P("section", "dp", None)
    norms = P("section", None, "dp")
    into = P("section", "expert", "dp", None)
    back = P("section", "expert", None, "dp")
    return jax.shard_map(
        shards,
        mesh=mesh,
        in_specs=(tokens, tokens, rows, rows, rows, norms, into, back, tables, tables, tables),
        out_specs=(tables, tables, rows, rows, rows, norms, into, back),
        check_vma=False,
    )
```
